256 devices in a mesh: day: 8 (over x, core), tile: 32 (over z, y).
Axes of the slice: x: 4, y: 4, z: 8, core: 2. Of those that a mesh axis runs over, the one named last changes fastest.
Arguments:
- seeds: bfloat16 [8, 65536, 128], P('day', 'tile'), may hold values from -6 to 6
- blocks: bfloat16 [8, 512, 3, 128, 128], P('day', 'tile'), may hold values from -0.3125 to 0.3125
- dest_tiles: int32 [8, 512, 3], P('day', 'tile'), may hold values from 0 to 511, as said below
Outputs:
- ftle: float32 [8, 64, 65536], P('day', None, 'tile')
- minor: float32 [8, 64, 65536], P('day', None, 'tile')
The draws below stay inside these ranges and needn't reach their ends.
Inputs may be any that keep to these rules, and one draw needn't show every extreme that they name: dest_tiles[d, t, 0] = t. For each section and each aligned block of 16 tiles, at most one of its blocks names a tile of any one other aligned block; in each section some aligned block names a tile in every other aligned block. The other destinations lie in the source tile's own aligned block.
All inputs are finite; a program needn't handle non-finite values.
Results may differ from the reference program's by a relative error of at most 0.035.
Values may be sent and summed in bfloat16 or wider, within the bound.
No kernel may reach another device: no remote copies, remote signals or barrier semaphores. Data moves between devices by JAX's collectives and lax.ppermute only.
A program may use at most 64 MiB of HBM per device.

```python
import jax
import jax.numpy as jnp
from jax import lax

TILE_PTS = 128
NNZ = 3
MEMBERS = 64
CH = 128
S_DEV = 1
STARTS = 8
TILES_DEV = 16
TILES = 512
POINTS = 65536
N_DAY = 8
N_TILE = 32


def draw_dest_tiles(key, part):
    key = jax.random.fold_in(key, 11)
    spare = TILES_DEV * (NNZ - 1)

    def one_device(sub_key, device, count):
        k_peer, k_slot, k_local = jax.random.split(sub_key, 3)
        others = (device + 1 + jax.random.permutation(k_peer, N_TILE - 1)) % N_TILE
        order = jax.random.permutation(k_slot, spare)
        rank = jnp.argsort(order).astype(jnp.int32)
        picked = others[jnp.minimum(rank, N_TILE - 2)]
        owner = jnp.where(rank < count, picked, device)
        local = jax.random.randint(k_local, (spare,), 0, TILES_DEV)
        offdiag = (owner * TILES_DEV + local).reshape(TILES_DEV, NNZ - 1)
        own = device * TILES_DEV + jnp.arange(TILES_DEV, dtype=jnp.int32)
        return jnp.concatenate([own[:, None], offdiag], axis=1).astype(jnp.int32)

    def one_day(day_key):
        k_full, k_count, k_dev = jax.random.split(day_key, 3)
        full = jax.random.randint(k_full, (), 0, N_TILE)
        counts = jax.random.randint(k_count, (N_TILE,), 1, N_TILE)
        devices = jnp.arange(N_TILE, dtype=jnp.int32)
        counts = jnp.where(devices == full, N_TILE - 1, counts)
        keys = jax.random.split(k_dev, N_TILE)
        table = jax.vmap(one_device)(keys, devices, counts)
        return table.reshape(TILES, NNZ)
    return jax.vmap(one_day)(jax.random.split(key, N_DAY)).astype(jnp.int32)


def steps_of(own_key, extent, shards, smallest, high):
    gain, own = 1.0, jax.random.fold_in(own_key, 6)
    for dim, blocks in shards:
        heights = jnp.exp(jax.random.uniform(jax.random.fold_in(own, dim), (blocks,), jnp.float32, smallest / len(shards), high / len(shards)))
        gain = gain * jnp.repeat(heights, extent[dim] // blocks).reshape([-1 if axis == dim else 1 for axis in range(len(extent))])
    return gain


def bell_draw(rng, dims, deviation, limit, cuts=(), kind=jnp.bfloat16):
    array = deviation * jax.random.normal(rng, dims, jnp.float32)
    if cuts:
        array = array * steps_of(rng, dims, cuts, -0.22, 0.18)
    return jnp.clip(array, -limit, limit).astype(kind)


def setup_inputs(seed: int = 0) -> dict:
    streams_of = jax.random.split(jax.random.key(seed), 4)
    return {
        "seeds": bell_draw(streams_of[0], (STARTS, POINTS, CH), 1.0, 6.0, ((0, 8), (1, 32))),
        "blocks": bell_draw(streams_of[1], (N_DAY, TILES, NNZ, TILE_PTS, TILE_PTS), (TILE_PTS * NNZ) ** -0.5, 0.3125, ((0, 8), (1, 32))),
        "dest_tiles": draw_dest_tiles(jax.random.fold_in(streams_of[3], 71), 0),
    }


def apply_section(state, wsec, dsec):
    prods = jnp.einsum('jkab,jbc->jkac', wsec.astype(jnp.float32), state.astype(jnp.float32))
    home = (jnp.arange(TILES, dtype=jnp.int32) // TILES_DEV)[:, None]
    remote = dsec // TILES_DEV != home
    rounded = lax.optimization_barrier(prods.astype(jnp.bfloat16)).astype(jnp.float32)
    prods = jnp.where(remote[:, :, None, None], rounded, prods)
    total = jax.ops.segment_sum(prods.reshape(TILES * NNZ, TILE_PTS, CH), dsec.reshape(TILES * NNZ), num_segments=TILES)
    return total.astype(jnp.bfloat16)

def diff_axis(field, axis):
    n = field.shape[axis]
    take = lambda lo, hi: lax.slice_in_dim(field, lo, hi, axis=axis)
    first = take(1, 2) - take(0, 1)
    middle = (take(2, n) - take(0, n - 2)) * 0.5
    last = take(n - 1, n) - take(n - 2, n - 1)
    return jnp.concatenate([first, middle, last], axis=axis)

def stretch_fields(final, dx, dy):
    a = dx[..., :MEMBERS]
    c = dx[..., MEMBERS:]
    b = dy[..., :MEMBERS]
    e = dy[..., MEMBERS:]
    c11 = a * a + c * c
    c12 = a * b + c * e
    c22 = b * b + e * e
    major = 0.5 * (c11 + c22 + jnp.sqrt((c11 - c22) ** 2 + 4.0 * c12 * c12))
    lead = jnp.maximum(major, 1.0)
    ftle = jnp.log(lead) / (2.0 * final)
    minor = (a * e - b * c) ** 2 / lead
    return (ftle, minor)

def reference(seeds, blocks, dest_tiles):

    def one_start(s):
        state = seeds[s].reshape(TILES, TILE_PTS, CH)
        group = s // S_DEV

        def step(carry, i):
            sec = ((group + i) % N_DAY).astype(jnp.int32)
            wsec = lax.dynamic_index_in_dim(blocks, sec, 0, False)
            dsec = lax.dynamic_index_in_dim(dest_tiles, sec, 0, False)
            return (apply_section(carry, wsec, dsec), None)
        final, _ = lax.scan(step, state, jnp.arange(N_DAY, dtype=jnp.int32))
        field = final.astype(jnp.float32)
        dx = diff_axis(field, 1)
        dy = diff_axis(field, 0)
        ftle, minor = stretch_fields(float(N_DAY), dx, dy)
        ftle = jnp.transpose(ftle, (2, 0, 1)).reshape(MEMBERS, POINTS)
        minor = jnp.transpose(minor, (2, 0, 1)).reshape(MEMBERS, POINTS)
        return (ftle, minor)
    ftle, minor = lax.map(one_start, jnp.arange(STARTS, dtype=jnp.int32))
    return (ftle, minor)
```

```python
import functools

import jax
import jax.numpy as jnp
from jax import lax
from jax.experimental import pallas as pl
from jax.experimental.pallas import tpu as pltpu
from jax.sharding import PartitionSpec as P

CHAINS = 1


def shifted(n, by):
    return [(i, (i + by) % n) for i in range(n)]


def step_kernel(first, chain, chains, tables, state_ref, arrived_ref, blocks_ref, out_ref, local_ref, state_scr, prods):
    tiles, nnz = blocks_ref.shape[0], blocks_ref.shape[1]
    peers, rows, points = out_ref.shape
    if first:
        half = rows // 2
        members = state_ref.shape[2] // 2
        for t in range(tiles):
            turned = jnp.transpose(state_ref[t].astype(jnp.float32)).astype(jnp.bfloat16)
            if chains == 1:
                state_scr[t] = turned
            else:
                state_scr[t, :half] = turned[chain * half : (chain + 1) * half]
                state_scr[t, half:] = turned[members + chain * half : members + (chain + 1) * half]
    else:
        summed_state(tables, state_ref, arrived_ref, state_scr)
    for t in range(tiles):
        v = state_scr[t]
        for k in range(nnz):
            p = lax.dot_general(
                v, blocks_ref[t, k], (((1,), (1,)), ((), ())), preferred_element_type=jnp.float32
            )
            if k == 0:
                local_ref[t] = p
            else:
                prods[t * (nnz - 1) + k - 1] = p
    for p in range(peers):
        out_ref[p] = prods[tables[0, p]].astype(jnp.bfloat16)
    for q in range(tiles * (nnz - 1)):
        home = tables[1, q]
        local_ref[home] = local_ref[home] + prods[q]


def summed_state(tables, total_ref, arrived_ref, state_scr):
    tiles = state_scr.shape[0]
    for p in range(arrived_ref.shape[0]):
        home = tables[2, p]
        total_ref[home] = total_ref[home] + arrived_ref[p].astype(jnp.float32)
    for t in range(tiles):
        state_scr[t] = total_ref[t].astype(jnp.bfloat16)


def first_body(chain, chains, tables, seeds_ref, blocks_ref, out_ref, local_ref, state_scr, prods):
    step_kernel(True, chain, chains, tables, seeds_ref, None, blocks_ref, out_ref, local_ref, state_scr, prods)


def later_body(tables, total_ref, arrived_ref, blocks_ref, out_ref, local_ref, state_scr, prods, total_scr):
    total_scr[...] = total_ref[...]
    step_kernel(False, 0, 0, tables, total_scr, arrived_ref, blocks_ref, out_ref, local_ref, state_scr, prods)


VMEM = pl.BlockSpec(memory_space=pltpu.VMEM)
SMEM = pl.BlockSpec(memory_space=pltpu.SMEM)


def one_step(tables, carried, blocks, peers, rows, chain=None, chains=None):
    tiles, nnz, points = blocks.shape[:3]
    outs = (
        jax.ShapeDtypeStruct((peers, rows, points), jnp.bfloat16),
        jax.ShapeDtypeStruct((tiles + 1, rows, points), jnp.float32),
    )
    scratch = [
        pltpu.VMEM((tiles, rows, points), jnp.bfloat16),
        pltpu.VMEM((tiles * (nnz - 1), rows, points), jnp.float32),
    ]
    if chain is None:
        body = later_body
        scratch.append(pltpu.VMEM((tiles + 1, rows, points), jnp.float32))
    else:
        body = functools.partial(first_body, chain, chains)
    return pl.pallas_call(
        body,
        out_shape=outs,
        in_specs=[SMEM] + [VMEM] * (len(carried) + 1),
        out_specs=(VMEM, VMEM),
        scratch_shapes=scratch,
        compiler_params=pltpu.CompilerParams(vmem_limit_bytes=32 * 1024 * 1024),
        cost_estimate=pl.CostEstimate(flops=2 * tiles * nnz * points * points * rows, bytes_accessed=4 << 20, transcendentals=0),
    )(tables, *carried, blocks)


def last_sum_body(tables, total_ref, arrived_ref, final_ref, total_scr):
    total_scr[...] = total_ref[...]
    summed_state(tables, total_scr, arrived_ref, final_ref)


def last_sum(tables, total, arrived):
    tiles, rows, points = total.shape[0] - 1, total.shape[1], total.shape[2]
    return pl.pallas_call(
        last_sum_body,
        out_shape=jax.ShapeDtypeStruct((tiles, rows, points), jnp.bfloat16),
        in_specs=[SMEM, VMEM, VMEM],
        out_specs=VMEM,
        scratch_shapes=[pltpu.VMEM(total.shape, jnp.float32)],
        compiler_params=pltpu.CompilerParams(vmem_limit_bytes=32 * 1024 * 1024),
    )(tables, total, arrived)


def stretch_body(ndays, place, final_ref, low_ref, high_ref, ftle_ref, minor_ref):
    tiles, rows, points = final_ref.shape
    half = rows // 2
    at_first, at_last = place[0] == 1, place[1] == 1
    lane = lax.broadcasted_iota(jnp.int32, (rows, points), 1)
    for t in range(tiles):
        here = final_ref[t].astype(jnp.float32)
        below = (final_ref[t - 1] if t > 0 else low_ref[0]).astype(jnp.float32)
        above = (final_ref[t + 1] if t < tiles - 1 else high_ref[0]).astype(jnp.float32)
        right = pltpu.roll(here, points - 1, 1)
        left = pltpu.roll(here, 1, 1)
        dx = jnp.where(lane == 0, right - here, jnp.where(lane == points - 1, here - left, (right - left) * 0.5))
        dy = (above - below) * 0.5
        if t == 0:
            dy = jnp.where(at_first, above - here, dy)
        if t == tiles - 1:
            dy = jnp.where(at_last, here - below, dy)
        a, c = dx[:half], dx[half:]
        b, e = dy[:half], dy[half:]
        c11 = a * a + c * c
        c12 = a * b + c * e
        c22 = b * b + e * e
        gap = c11 - c22
        major = 0.5 * (c11 + c22 + jnp.sqrt(gap * gap + 4.0 * c12 * c12))
        lead = jnp.maximum(major, 1.0)
        det = a * e - b * c
        at = slice(t * points, (t + 1) * points)
        ftle_ref[:, at] = jnp.log(lead) / (2.0 * ndays)
        minor_ref[:, at] = det * det / lead


def stretch(place, final, low, high, ndays):
    tiles, rows, points = final.shape
    shape = jax.ShapeDtypeStruct((rows // 2, tiles * points), jnp.float32)
    return pl.pallas_call(
        functools.partial(stretch_body, float(ndays)),
        out_shape=(shape, shape),
        in_specs=[SMEM, VMEM, VMEM, VMEM],
        out_specs=(VMEM, VMEM),
        compiler_params=pltpu.CompilerParams(vmem_limit_bytes=32 * 1024 * 1024),
    )(place, final, low, high)


def sending_tables(own, me, tiles, peers, nnz):
    off = own.reshape(own.shape[0], tiles, nnz)[:, :, 1:].reshape(own.shape[0], tiles * (nnz - 1))
    dev, loc = off // tiles, off % tiles
    peer = jnp.arange(peers, dtype=jnp.int32)
    order = jnp.arange(tiles * (nnz - 1), dtype=jnp.int32)
    match = dev[:, None, :] == peer[None, :, None]
    for_peer = jnp.max(jnp.where(match, order, 0), axis=2)
    home = jnp.where(dev == me, loc, tiles)
    return for_peer, home


def body(seeds, blocks, dest_tiles):
    tiles, nnz, points = blocks.shape[1:4]
    width = seeds.shape[2]
    ndays, peers = lax.axis_size("day"), lax.axis_size("tile")
    me, day = lax.axis_index("tile"), lax.axis_index("day")
    rows = width // CHAINS
    off = tiles * (nnz - 1)

    own_first = sending_tables(dest_tiles.reshape(1, tiles * nnz), me, tiles, peers, nnz)
    first_table = jnp.concatenate([own_first[0], own_first[1], jnp.zeros_like(own_first[0])], axis=0)

    everyone = lax.all_gather(dest_tiles.reshape(tiles * nnz), ("day", "tile"), axis=0, tiled=False)
    everyone = everyone.reshape(ndays, peers, tiles * nnz)
    everyone = jnp.roll(everyone, -day, axis=0)
    own = lax.dynamic_index_in_dim(everyone, me, 1, keepdims=False)
    for_peer, home = sending_tables(own, me, tiles, peers, nnz)
    peer = jnp.arange(peers, dtype=jnp.int32)
    reaches = (everyone // tiles == me) & (peer != me)[None, :, None]
    landing = jnp.max(jnp.where(reaches, everyone % tiles, -1), axis=2)
    landing = jnp.where(landing < 0, tiles, landing)
    tables = jnp.stack([for_peer[1:], home[1:], landing[:-1]], axis=1)
    last_table = jnp.stack([for_peer[0], home[0], landing[-1]], axis=0)

    seeds = seeds.reshape(tiles, points, width)
    wblk = blocks[0]
    nxt = None
    chains = [None] * CHAINS
    for step in range(ndays):
        if step < ndays - 1:
            nxt = lax.ppermute(wblk, "day", shifted(ndays, -1))
        for c in range(CHAINS):
            if step == 0:
                out, local = one_step(first_table, (seeds,), wblk, peers, rows, c, CHAINS)
            else:
                out, local = one_step(tables[step - 1], chains[c], wblk, peers, rows)
            arrived = lax.all_to_all(out, "tile", split_axis=0, concat_axis=0, tiled=True)
            chains[c] = (local, arrived)
        wblk = nxt
    place = jnp.stack([me == 0, me == peers - 1]).astype(jnp.int32)
    ftles, minors = [], []
    for c in range(CHAINS):
        final = last_sum(last_table, *chains[c])
        low = lax.ppermute(final[-1:], "tile", [(i, i + 1) for i in range(peers - 1)])
        high = lax.ppermute(final[:1], "tile", [(i + 1, i) for i in range(peers - 1)])
        f, m = stretch(place, final, low, high, ndays)
        ftles.append(f)
        minors.append(m)
    if CHAINS == 1:
        return ftles[0][None], minors[0][None]
    return jnp.concatenate(ftles, axis=0)[None], jnp.concatenate(minors, axis=0)[None]


def solution(mesh):
    in_specs = (P("day", "tile", None), P("day", "tile", None, None, None), P("day", "tile", None))
    out_specs = (P("day", None, "tile"), P("day", None, "tile"))
    return jax.shard_map(body, mesh=mesh, in_specs=in_specs, out_specs=out_specs, check_vma=False)
```

```python
import functools

import jax
import jax.numpy as jnp
from jax import lax
from jax.experimental import pallas as pl
from jax.experimental.pallas import tpu as pltpu
from jax.sharding import PartitionSpec as P

VMEM = pl.BlockSpec(memory_space=pltpu.VMEM)
SMEM = pl.BlockSpec(memory_space=pltpu.SMEM)
HBM = pl.BlockSpec(memory_space=pltpu.HBM)
PARAMS = pltpu.CompilerParams(vmem_limit_bytes=56 * 1024 * 1024)
SMALL = pltpu.CompilerParams(vmem_limit_bytes=16 * 1024 * 1024)
PART = 8
BLOCK, SOURCE, HOME, LANDING = range(4)


def shifted(n, by):
    return [(i, (i + by) % n) for i in range(n)]


def product(v, block):
    return lax.dot_general(v, block, (((1,), (1,)), ((), ())), preferred_element_type=jnp.float32)


def send_products(table, state_ref, blocks_scr, out_ref, stage, out_sems):
    peers = stage.shape[0]
    copies = []
    for p in range(peers):
        v = state_ref[table[SOURCE, p]]
        stage[p] = product(v, blocks_scr[table[BLOCK, p]]).astype(jnp.bfloat16)
        if p % PART == PART - 1:
            part = pl.ds(p + 1 - PART, PART)
            copy = pltpu.make_async_copy(stage.at[part], out_ref.at[part], out_sems.at[p // PART])
            copy.start()
            copies.append(copy)
    for copy in copies:
        copy.wait()


def arrival_copies(arrived_ref, arrived_scr, sems):
    parts = [pl.ds(p, PART) for p in range(0, arrived_scr.shape[0], PART)]
    return [
        pltpu.make_async_copy(arrived_ref.at[part], arrived_scr.at[part], sems.at[n]) for n, part in enumerate(parts)
    ]


def add_arrived(table, copies, arrived_scr, gathered):
    gathered[...] = jnp.zeros_like(gathered)
    for n, copy in enumerate(copies):
        copy.wait()
        for p in range(n * PART, (n + 1) * PART):
            home = table[LANDING, p]
            gathered[home] = gathered[home] + arrived_scr[p].astype(jnp.float32)


def first_body(table, seeds_ref, blocks_ref, out_ref, state_ref, blocks_scr, stage, state_scr, sems, out_sems):
    load = pltpu.make_async_copy(blocks_ref, blocks_scr, sems.at[0])
    load.start()
    for t in range(state_scr.shape[0]):
        state_scr[t] = jnp.transpose(seeds_ref[t].astype(jnp.float32)).astype(jnp.bfloat16)
    store = pltpu.make_async_copy(state_scr, state_ref, sems.at[2])
    store.start()
    load.wait()
    send_products(table, state_scr, blocks_scr, out_ref, stage, out_sems)
    store.wait()


def send_body(
    before, table, arrived_ref, local_ref, blocks_ref, out_ref, state_ref,
    blocks_scr, stage, state_scr, arrived_scr, gathered, local_scr, sems, out_sems, in_sems,
):
    arrivals = arrival_copies(arrived_ref, arrived_scr, in_sems)
    load_local = pltpu.make_async_copy(local_ref, local_scr, sems.at[1])
    load = pltpu.make_async_copy(blocks_ref, blocks_scr, sems.at[0])
    for copy in [*arrivals, load_local, load]:
        copy.start()
    add_arrived(before, arrivals, arrived_scr, gathered)
    load_local.wait()
    for t in range(state_scr.shape[0]):
        state_scr[t] = (gathered[t] + local_scr[t]).astype(jnp.bfloat16)
    store = pltpu.make_async_copy(state_scr, state_ref, sems.at[2])
    store.start()
    load.wait()
    send_products(table, state_scr, blocks_scr, out_ref, stage, out_sems)
    store.wait()


def send(tables, carried, blocks, peers):
    points = blocks.shape[1]
    first = len(carried) == 1
    rows = points
    tiles = carried[-1].shape[0]
    scratch = [
        pltpu.VMEM(blocks.shape, jnp.bfloat16),
        pltpu.VMEM((peers, rows, points), jnp.bfloat16),
        pltpu.VMEM((tiles, rows, points), jnp.bfloat16),
    ]
    if not first:
        scratch += [
            pltpu.VMEM((peers, rows, points), jnp.bfloat16),
            pltpu.VMEM((tiles + 1, rows, points), jnp.float32),
            pltpu.VMEM((tiles, rows, points), jnp.float32),
        ]
    scratch += [pltpu.SemaphoreType.DMA((3,)), pltpu.SemaphoreType.DMA((peers // PART,))]
    if not first:
        scratch.append(pltpu.SemaphoreType.DMA((peers // PART,)))
    return pl.pallas_call(
        first_body if first else send_body,
        out_shape=(
            jax.ShapeDtypeStruct((peers, rows, points), jnp.bfloat16),
            jax.ShapeDtypeStruct((tiles, rows, points), jnp.bfloat16),
        ),
        in_specs=[SMEM] * len(tables) + ([VMEM] if first else [HBM, HBM]) + [HBM],
        out_specs=(HBM, HBM),
        scratch_shapes=scratch,
        compiler_params=PARAMS,
        cost_estimate=pl.CostEstimate(
            flops=2 * peers * points * points * rows, bytes_accessed=4 << 20, transcendentals=0
        ),
    )(*tables, *carried, blocks)


def keep_body(table, state_ref, blocks_ref, local_ref, total, sem):
    tiles = state_ref.shape[0]
    nnz = blocks_ref.shape[0] // tiles
    for t in range(tiles):
        total[t] = product(state_ref[t], blocks_ref[t * nnz])
    for t in range(tiles):
        for k in range(nnz - 1):
            home = table[HOME, t * (nnz - 1) + k]
            total[home] = total[home] + product(state_ref[t], blocks_ref[t * nnz + 1 + k])
    store = pltpu.make_async_copy(total.at[pl.ds(0, tiles)], local_ref, sem)
    store.start()
    store.wait()


def keep(table, state, blocks):
    tiles, rows, points = state.shape
    return pl.pallas_call(
        keep_body,
        out_shape=jax.ShapeDtypeStruct((tiles, rows, points), jnp.float32),
        in_specs=[SMEM, VMEM, VMEM],
        out_specs=HBM,
        scratch_shapes=[pltpu.VMEM((tiles + 1, rows, points), jnp.float32), pltpu.SemaphoreType.DMA],
        compiler_params=PARAMS,
        cost_estimate=pl.CostEstimate(
            flops=2 * blocks.shape[0] * points * points * rows, bytes_accessed=4 << 20, transcendentals=0
        ),
    )(table, state, blocks)


def last_body(before, arrived_ref, local_ref, final_ref, edges_ref, arrived_scr, gathered, local_scr, sem, in_sems):
    arrivals = arrival_copies(arrived_ref, arrived_scr, in_sems)
    load_local = pltpu.make_async_copy(local_ref, local_scr, sem)
    for copy in [*arrivals, load_local]:
        copy.start()
    add_arrived(before, arrivals, arrived_scr, gathered)
    load_local.wait()
    tiles = final_ref.shape[0]
    for t in range(tiles):
        final_ref[t] = (gathered[t] + local_scr[t]).astype(jnp.bfloat16)
    edges_ref[0] = final_ref[0]
    edges_ref[1] = final_ref[tiles - 1]


def last_sum(before, arrived, local):
    tiles, rows, points = local.shape
    return pl.pallas_call(
        last_body,
        out_shape=(
            jax.ShapeDtypeStruct((tiles, rows, points), jnp.bfloat16),
            jax.ShapeDtypeStruct((2, rows, points), jnp.bfloat16),
        ),
        in_specs=[SMEM, HBM, HBM],
        out_specs=(VMEM, VMEM),
        scratch_shapes=[
            pltpu.VMEM(arrived.shape, jnp.bfloat16),
            pltpu.VMEM((tiles + 1, rows, points), jnp.float32),
            pltpu.VMEM((tiles, rows, points), jnp.float32),
            pltpu.SemaphoreType.DMA,
            pltpu.SemaphoreType.DMA((arrived.shape[0] // PART,)),
        ],
        compiler_params=SMALL,
    )(before, arrived, local)


def stretch_tile(ndays, here, dy):
    rows, points = here.shape
    half = rows // 2
    lane = lax.broadcasted_iota(jnp.int32, (rows, points), 1)
    right = pltpu.roll(here, points - 1, 1)
    left = pltpu.roll(here, 1, 1)
    dx = jnp.where(lane == 0, right - here, jnp.where(lane == points - 1, here - left, (right - left) * 0.5))
    a, c = dx[:half], dx[half:]
    b, e = dy[:half], dy[half:]
    c11 = a * a + c * c
    c12 = a * b + c * e
    c22 = b * b + e * e
    gap = c11 - c22
    major = 0.5 * (c11 + c22 + jnp.sqrt(gap * gap + 4.0 * c12 * c12))
    lead = jnp.maximum(major, 1.0)
    det = a * e - b * c
    return jnp.log(lead) / (2.0 * ndays), det * det / lead


def inner_body(ndays, final_ref, ftle_ref, minor_ref):
    tiles, rows, points = final_ref.shape
    for t in range(1, tiles - 1):
        here = final_ref[t].astype(jnp.float32)
        dy = (final_ref[t + 1].astype(jnp.float32) - final_ref[t - 1].astype(jnp.float32)) * 0.5
        at = slice(t * points, (t + 1) * points)
        ftle_ref[:, at], minor_ref[:, at] = stretch_tile(ndays, here, dy)


def edge_body(ndays, place, final_ref, low_ref, high_ref, ftle_in, minor_in, ftle_ref, minor_ref, ftle_scr, minor_scr, sems):
    tiles, rows, points = final_ref.shape
    copies = []
    for i, t in enumerate((0, tiles - 1)):
        here = final_ref[t].astype(jnp.float32)
        below = (final_ref[t - 1] if t > 0 else low_ref[0]).astype(jnp.float32)
        above = (final_ref[t + 1] if t < tiles - 1 else high_ref[0]).astype(jnp.float32)
        one_sided = above - here if t == 0 else here - below
        dy = jnp.where(place[i] == 1, one_sided, (above - below) * 0.5)
        ftle_scr[i], minor_scr[i] = stretch_tile(ndays, here, dy)
        at = pl.ds(t * points, points)
        for n, (scr, ref) in enumerate(((ftle_scr, ftle_ref), (minor_scr, minor_ref))):
            copy = pltpu.make_async_copy(scr.at[i], ref.at[:, at], sems.at[2 * i + n])
            copy.start()
            copies.append(copy)
    for copy in copies:
        copy.wait()


def stretch_inner(final, ndays):
    tiles, rows, points = final.shape
    shape = jax.ShapeDtypeStruct((rows // 2, tiles * points), jnp.float32)
    return pl.pallas_call(
        functools.partial(inner_body, float(ndays)),
        out_shape=(shape, shape),
        in_specs=[VMEM],
        out_specs=(VMEM, VMEM),
        compiler_params=SMALL,
        cost_estimate=pl.CostEstimate(flops=40 * rows * tiles * points, bytes_accessed=2 << 20, transcendentals=0),
    )(final)


def stretch_edges(place, final, low, high, inner, ndays):
    tiles, rows, points = final.shape
    shape = jax.ShapeDtypeStruct((rows // 2, tiles * points), jnp.float32)
    scr = pltpu.VMEM((2, rows // 2, points), jnp.float32)
    return pl.pallas_call(
        functools.partial(edge_body, float(ndays)),
        out_shape=(shape, shape),
        in_specs=[SMEM, VMEM, VMEM, VMEM, HBM, HBM],
        out_specs=(HBM, HBM),
        scratch_shapes=[scr, scr, pltpu.SemaphoreType.DMA((4,))],
        input_output_aliases={4: 0, 5: 1},
        compiler_params=SMALL,
    )(place, final, low, high, *inner)


def own_rows(dest, me, tiles, peers, nnz):
    flat = dest.reshape(tiles * nnz)
    off = dest[:, 1:].reshape(tiles * (nnz - 1))
    peer = jnp.arange(peers, dtype=jnp.int32)
    order = jnp.arange(tiles * nnz, dtype=jnp.int32)
    block = jnp.max(jnp.where(flat[None, :] // tiles == peer[:, None], order, 0), axis=1)
    home = jnp.where(off // tiles == me, off % tiles, tiles)
    return block, block // nnz, home


def landing_row(dest, me, tiles, peers):
    known = dest.reshape(1, -1)
    step = 1
    while step < peers:
        known = jnp.concatenate([known, lax.ppermute(known, "tile", [(i, i ^ step) for i in range(peers)])], axis=0)
        step *= 2
    row_of = jnp.arange(peers, dtype=jnp.int32)
    lands = jnp.max(jnp.where(known // tiles == me, known % tiles, -1), axis=1)
    lands = jnp.where((lands < 0) | (row_of == 0), tiles, lands)
    match = (row_of[:, None] ^ row_of[None, :]) == me
    return jnp.sum(jnp.where(match, lands[None, :], 0), axis=1)


def body(seeds, blocks, dest_tiles):
    tiles, nnz, points = blocks.shape[1:4]
    width = seeds.shape[2]
    ndays, peers = lax.axis_size("day"), lax.axis_size("tile")
    me = lax.axis_index("tile")

    block, source, home = own_rows(dest_tiles[0], me, tiles, peers, nnz)
    first_table = jnp.stack([block, source, home, jnp.zeros_like(home)])
    table = first_table
    seeds = seeds.reshape(tiles, points, width)
    wblk = blocks.reshape(tiles * nnz, points, points)

    for step in range(ndays):
        if step == 0:
            out, state = send((first_table,), (seeds,), wblk, peers)
        else:
            out, state = send((before, table), (arrived, local), wblk, peers)
        arrived = lax.all_to_all(out, "tile", split_axis=0, concat_axis=0, tiled=True)
        local = keep(table, state, wblk)
        if step == 0:
            dest, local = lax.optimization_barrier((dest_tiles[0], local))
            landing = landing_row(dest, me, tiles, peers)
            table = jnp.stack([block, source, home, landing])
        before = table
        if step < ndays - 1:
            table = lax.ppermute(table, "day", shifted(ndays, -1))
            wblk = lax.ppermute(wblk, "day", shifted(ndays, -1))
    final, edges = last_sum(before, arrived, local)
    low = lax.ppermute(edges[1:], "tile", [(i, i + 1) for i in range(peers - 1)])
    high = lax.ppermute(edges[:1], "tile", [(i + 1, i) for i in range(peers - 1)])
    place = jnp.stack([me == 0, me == peers - 1]).astype(jnp.int32)
    inner = stretch_inner(final, ndays)
    ftle, minor = stretch_edges(place, final, low, high, inner, ndays)
    return ftle[None], minor[None]


def solution(mesh):
    in_specs = (P("day", "tile", None), P("day", "tile", None, None, None), P("day", "tile", None))
    out_specs = (P("day", None, "tile"), P("day", None, "tile"))
    return jax.shard_map(body, mesh=mesh, in_specs=in_specs, out_specs=out_specs, check_vma=False)
```

```python
import functools

import jax
import jax.numpy as jnp
from jax import lax
from jax.experimental import pallas as pl
from jax.experimental.pallas import tpu as pltpu
from jax.sharding import PartitionSpec as P

VMEM = pl.BlockSpec(memory_space=pltpu.VMEM)
SMEM = pl.BlockSpec(memory_space=pltpu.SMEM)
HBM = pl.BlockSpec(memory_space=pltpu.HBM)
PARAMS = pltpu.CompilerParams(vmem_limit_bytes=56 * 1024 * 1024)
SMALL = pltpu.CompilerParams(vmem_limit_bytes=16 * 1024 * 1024)
PART = 8
WANTED, HOME, LANDING = range(3)


def shifted(n, by):
    return [(i, (i + by) % n) for i in range(n)]


def product(v, block):
    return lax.dot_general(v, block, (((1,), (1,)), ((), ())), preferred_element_type=jnp.float32)


def send_products(wanted, state_scr, blocks_scr, out_ref, made, stage, out_sems):
    tiles = state_scr.shape[0]
    nnz = blocks_scr.shape[0] // tiles
    for t in range(tiles):
        v = state_scr[t]
        for k in range(1, nnz):
            made[t * (nnz - 1) + k - 1] = product(v, blocks_scr[t * nnz + k]).astype(jnp.bfloat16)
    copies = []
    for p in range(stage.shape[0]):
        stage[p] = made[wanted(p)]
        if p % PART == PART - 1:
            part = pl.ds(p + 1 - PART, PART)
            copy = pltpu.make_async_copy(stage.at[part], out_ref.at[part], out_sems.at[p // PART])
            copy.start()
            copies.append(copy)
    for copy in copies:
        copy.wait()


def add_arrived(table, arrived_ref, gathered):
    gathered[...] = jnp.zeros_like(gathered)
    for p in range(arrived_ref.shape[0]):
        home = table[LANDING, p]
        gathered[home] = gathered[home] + arrived_ref[p].astype(jnp.float32)


def first_body(dest, seeds_ref, blocks_ref, out_ref, state_ref, blocks_scr, made, stage, state_scr, numbers, sems, out_sems):
    load = pltpu.make_async_copy(blocks_ref, blocks_scr, sems.at[0])
    load.start()
    tiles, nnz = dest.shape[1:]
    for t in range(tiles):
        state_scr[t] = jnp.transpose(seeds_ref[t].astype(jnp.float32)).astype(jnp.bfloat16)
    store = pltpu.make_async_copy(state_scr, state_ref, sems.at[2])
    store.start()
    for p in range(stage.shape[0]):
        numbers[p] = 0
    for t in range(tiles):
        for k in range(1, nnz):
            numbers[dest[0, t, k] // tiles] = t * (nnz - 1) + k - 1
    load.wait()
    send_products(lambda p: numbers[p], state_scr, blocks_scr, out_ref, made, stage, out_sems)
    store.wait()


def send_body(
    before, table, arrived_ref, local_ref, blocks_ref, out_ref, state_ref,
    blocks_scr, made, stage, state_scr, gathered, local_scr, sems, out_sems,
):
    load_local = pltpu.make_async_copy(local_ref, local_scr, sems.at[1])
    load = pltpu.make_async_copy(blocks_ref, blocks_scr, sems.at[0])
    load_local.start()
    load.start()
    add_arrived(before, arrived_ref, gathered)
    load_local.wait()
    for t in range(state_scr.shape[0]):
        state_scr[t] = (gathered[t] + local_scr[t]).astype(jnp.bfloat16)
    store = pltpu.make_async_copy(state_scr, state_ref, sems.at[2])
    store.start()
    load.wait()
    send_products(lambda p: table[WANTED, p], state_scr, blocks_scr, out_ref, made, stage, out_sems)
    store.wait()


def send(tables, carried, blocks, peers):
    count, points = blocks.shape[:2]
    first = len(carried) == 1
    rows = points
    tiles = carried[-1].shape[0]
    scratch = [
        pltpu.VMEM(blocks.shape, jnp.bfloat16),
        pltpu.VMEM((count - tiles, rows, points), jnp.bfloat16),
        pltpu.VMEM((peers, rows, points), jnp.bfloat16),
        pltpu.VMEM((tiles, rows, points), jnp.bfloat16),
    ]
    if first:
        scratch.append(pltpu.SMEM((peers,), jnp.int32))
    else:
        scratch.append(pltpu.VMEM((tiles + 1, rows, points), jnp.float32))
        scratch.append(pltpu.VMEM((tiles, rows, points), jnp.float32))
    scratch += [pltpu.SemaphoreType.DMA((3,)), pltpu.SemaphoreType.DMA((peers // PART,))]
    return pl.pallas_call(
        first_body if first else send_body,
        out_shape=(
            jax.ShapeDtypeStruct((peers, rows, points), jnp.bfloat16),
            jax.ShapeDtypeStruct((tiles, rows, points), jnp.bfloat16),
        ),
        in_specs=[SMEM] * len(tables) + ([VMEM] if first else [VMEM, HBM]) + [HBM],
        out_specs=(HBM, HBM),
        scratch_shapes=scratch,
        compiler_params=PARAMS,
        cost_estimate=pl.CostEstimate(
            flops=2 * peers * points * points * rows, bytes_accessed=4 << 20, transcendentals=0
        ),
    )(*tables, *carried, blocks)


def keep_body(table, state_ref, blocks_ref, local_ref, total, sem):
    tiles = state_ref.shape[0]
    nnz = blocks_ref.shape[0] // tiles
    for t in range(tiles):
        total[t] = product(state_ref[t], blocks_ref[t * nnz])
    for t in range(tiles):
        for k in range(nnz - 1):
            home = table[HOME, t * (nnz - 1) + k]
            total[home] = total[home] + product(state_ref[t], blocks_ref[t * nnz + 1 + k])
    store = pltpu.make_async_copy(total.at[pl.ds(0, tiles)], local_ref, sem)
    store.start()
    store.wait()


def keep(table, state, blocks):
    tiles, rows, points = state.shape
    return pl.pallas_call(
        keep_body,
        out_shape=jax.ShapeDtypeStruct((tiles, rows, points), jnp.float32),
        in_specs=[SMEM, VMEM, VMEM],
        out_specs=HBM,
        scratch_shapes=[pltpu.VMEM((tiles + 1, rows, points), jnp.float32), pltpu.SemaphoreType.DMA],
        compiler_params=PARAMS,
        cost_estimate=pl.CostEstimate(
            flops=2 * blocks.shape[0] * points * points * rows, bytes_accessed=4 << 20, transcendentals=0
        ),
    )(table, state, blocks)


def last_body(before, arrived_ref, local_ref, final_ref, edges_ref, gathered, local_scr, sem):
    load_local = pltpu.make_async_copy(local_ref, local_scr, sem)
    load_local.start()
    add_arrived(before, arrived_ref, gathered)
    load_local.wait()
    tiles = final_ref.shape[0]
    for t in range(tiles):
        final_ref[t] = (gathered[t] + local_scr[t]).astype(jnp.bfloat16)
    edges_ref[0] = final_ref[0]
    edges_ref[1] = final_ref[tiles - 1]


def last_sum(before, arrived, local):
    tiles, rows, points = local.shape
    return pl.pallas_call(
        last_body,
        out_shape=(
            jax.ShapeDtypeStruct((tiles, rows, points), jnp.bfloat16),
            jax.ShapeDtypeStruct((2, rows, points), jnp.bfloat16),
        ),
        in_specs=[SMEM, VMEM, HBM],
        out_specs=(VMEM, VMEM),
        scratch_shapes=[
            pltpu.VMEM((tiles + 1, rows, points), jnp.float32),
            pltpu.VMEM((tiles, rows, points), jnp.float32),
            pltpu.SemaphoreType.DMA,
        ],
        compiler_params=SMALL,
    )(before, arrived, local)


def stretch_tile(ndays, here, dy):
    rows, points = here.shape
    half = rows // 2
    lane = lax.broadcasted_iota(jnp.int32, (rows, points), 1)
    right = pltpu.roll(here, points - 1, 1)
    left = pltpu.roll(here, 1, 1)
    dx = jnp.where(lane == 0, right - here, jnp.where(lane == points - 1, here - left, (right - left) * 0.5))
    a, c = dx[:half], dx[half:]
    b, e = dy[:half], dy[half:]
    c11 = a * a + c * c
    c12 = a * b + c * e
    c22 = b * b + e * e
    gap = c11 - c22
    major = 0.5 * (c11 + c22 + jnp.sqrt(gap * gap + 4.0 * c12 * c12))
    lead = jnp.maximum(major, 1.0)
    det = a * e - b * c
    return jnp.log(lead) / (2.0 * ndays), det * det / lead


def inner_body(ndays, final_ref, ftle_ref, minor_ref):
    tiles, rows, points = final_ref.shape
    for t in range(1, tiles - 1):
        here = final_ref[t].astype(jnp.float32)
        dy = (final_ref[t + 1].astype(jnp.float32) - final_ref[t - 1].astype(jnp.float32)) * 0.5
        at = slice(t * points, (t + 1) * points)
        ftle_ref[:, at], minor_ref[:, at] = stretch_tile(ndays, here, dy)


def edge_body(ndays, place, final_ref, low_ref, high_ref, ftle_in, minor_in, ftle_ref, minor_ref, ftle_scr, minor_scr, sems):
    tiles, rows, points = final_ref.shape
    copies = []
    for i, t in enumerate((0, tiles - 1)):
        here = final_ref[t].astype(jnp.float32)
        below = (final_ref[t - 1] if t > 0 else low_ref[0]).astype(jnp.float32)
        above = (final_ref[t + 1] if t < tiles - 1 else high_ref[0]).astype(jnp.float32)
        one_sided = above - here if t == 0 else here - below
        dy = jnp.where(place[i] == 1, one_sided, (above - below) * 0.5)
        ftle_scr[i], minor_scr[i] = stretch_tile(ndays, here, dy)
        at = pl.ds(t * points, points)
        for n, (scr, ref) in enumerate(((ftle_scr, ftle_ref), (minor_scr, minor_ref))):
            copy = pltpu.make_async_copy(scr.at[i], ref.at[:, at], sems.at[2 * i + n])
            copy.start()
            copies.append(copy)
    for copy in copies:
        copy.wait()


def stretch_inner(final, ndays):
    tiles, rows, points = final.shape
    shape = jax.ShapeDtypeStruct((rows // 2, tiles * points), jnp.float32)
    return pl.pallas_call(
        functools.partial(inner_body, float(ndays)),
        out_shape=(shape, shape),
        in_specs=[VMEM],
        out_specs=(VMEM, VMEM),
        compiler_params=SMALL,
        cost_estimate=pl.CostEstimate(flops=40 * rows * tiles * points, bytes_accessed=2 << 20, transcendentals=0),
    )(final)


def stretch_edges(place, final, low, high, inner, ndays):
    tiles, rows, points = final.shape
    shape = jax.ShapeDtypeStruct((rows // 2, tiles * points), jnp.float32)
    scr = pltpu.VMEM((2, rows // 2, points), jnp.float32)
    return pl.pallas_call(
        functools.partial(edge_body, float(ndays)),
        out_shape=(shape, shape),
        in_specs=[SMEM, VMEM, VMEM, VMEM, HBM, HBM],
        out_specs=(HBM, HBM),
        scratch_shapes=[scr, scr, pltpu.SemaphoreType.DMA((4,))],
        input_output_aliases={4: 0, 5: 1},
        compiler_params=SMALL,
    )(place, final, low, high, *inner)


def own_rows(dest, me, tiles, peers, nnz):
    off = dest[:, 1:].reshape(tiles * (nnz - 1))
    peer = jnp.arange(peers, dtype=jnp.int32)
    order = jnp.arange(tiles * (nnz - 1), dtype=jnp.int32)
    wanted = jnp.max(jnp.where(off[None, :] // tiles == peer[:, None], order, 0), axis=1)
    home = jnp.where(off // tiles == me, off % tiles, tiles)
    return wanted, home


def landing_row(dest, me, tiles, peers):
    known = dest.reshape(1, -1)
    step = 1
    while step < peers:
        known = jnp.concatenate([known, lax.ppermute(known, "tile", [(i, i ^ step) for i in range(peers)])], axis=0)
        step *= 2
    row_of = jnp.arange(peers, dtype=jnp.int32)
    lands = jnp.max(jnp.where(known // tiles == me, known % tiles, -1), axis=1)
    lands = jnp.where((lands < 0) | (row_of == 0), tiles, lands)
    match = (row_of[:, None] ^ row_of[None, :]) == me
    return jnp.sum(jnp.where(match, lands[None, :], 0), axis=1)


def body(seeds, blocks, dest_tiles):
    tiles, nnz, points = blocks.shape[1:4]
    width = seeds.shape[2]
    ndays, peers = lax.axis_size("day"), lax.axis_size("tile")
    me = lax.axis_index("tile")

    seeds = seeds.reshape(tiles, points, width)
    wblk = blocks.reshape(tiles * nnz, points, points)

    for step in range(ndays):
        if step == 0:
            out, state = send((dest_tiles,), (seeds,), wblk, peers)
        else:
            out, state = send((before, table), (arrived, local), wblk, peers)
        arrived = lax.all_to_all(out, "tile", split_axis=0, concat_axis=0, tiled=True)
        if step == 0:
            dest, state = lax.optimization_barrier((dest_tiles[0], state))
            landing = landing_row(dest, me, tiles, peers)
            table = jnp.stack([*own_rows(dest, me, tiles, peers, nnz), landing])
        local = keep(table, state, wblk)
        before = table
        if step < ndays - 1:
            table = lax.ppermute(table, "day", shifted(ndays, -1))
            wblk = lax.ppermute(wblk, "day", shifted(ndays, -1))
    final, edges = last_sum(before, arrived, local)
    low = lax.ppermute(edges[1:], "tile", [(i, i + 1) for i in range(peers - 1)])
    high = lax.ppermute(edges[:1], "tile", [(i + 1, i) for i in range(peers - 1)])
    place = jnp.stack([me == 0, me == peers - 1]).astype(jnp.int32)
    inner = stretch_inner(final, ndays)
    ftle, minor = stretch_edges(place, final, low, high, inner, ndays)
    return ftle[None], minor[None]


def solution(mesh):
    in_specs = (P("day", "tile", None), P("day", "tile", None, None, None), P("day", "tile", None))
    out_specs = (P("day", None, "tile"), P("day", None, "tile"))
    return jax.shard_map(body, mesh=mesh, in_specs=in_specs, out_specs=out_specs, check_vma=False)
```

```python
import functools

import jax
import jax.numpy as jnp
from jax import lax
from jax.experimental import pallas as pl
from jax.experimental.pallas import tpu as pltpu
from jax.sharding import PartitionSpec as P

VMEM = pl.BlockSpec(memory_space=pltpu.VMEM)
SMEM = pl.BlockSpec(memory_space=pltpu.SMEM)
HBM = pl.BlockSpec(memory_space=pltpu.HBM)
SEND_SPECS = [VMEM, VMEM, VMEM]
SEND = pltpu.CompilerParams(vmem_limit_bytes=24 * 1024 * 1024)
KEEP = pltpu.CompilerParams(vmem_limit_bytes=24 * 1024 * 1024)
SMALL = pltpu.CompilerParams(vmem_limit_bytes=16 * 1024 * 1024)
PART = 4
SAYS = 16
WANTED, HOME, LANDED = range(3)


def shifted(n, by):
    return [(i, (i + by) % n) for i in range(n)]


def product(v, block):
    return lax.dot_general(v, block, (((1,), (1,)), ((), ())), preferred_element_type=jnp.float32)


def send_products(wanted, block_of, state_ref, out_ref, stage, out_sems):
    rows, each = state_ref.shape[1], wanted.each
    copies = []
    for p in range(stage.shape[0]):
        number = wanted(p)
        stage[p, :rows] = product(state_ref[number // each], block_of(number)).astype(jnp.bfloat16)
        if p % PART == PART - 1:
            part = pl.ds(p + 1 - PART, PART)
            copy = pltpu.make_async_copy(stage.at[part], out_ref.at[part], out_sems.at[p // PART])
            copy.start()
            copies.append(copy)
    for copy in copies:
        copy.wait()


def add_arrived(table, arrived_ref, gathered):
    gathered[...] = jnp.zeros_like(gathered)
    rows = gathered.shape[1]
    for p in range(arrived_ref.shape[0]):
        home = table[LANDED, p]
        gathered[home] = gathered[home] + arrived_ref[p, :rows].astype(jnp.float32)


class Wanted:
    def __init__(self, read, each):
        self.read, self.each = read, each

    def __call__(self, p):
        return self.read(p)


def first_body(dest, seeds_ref, blocks_ref, out_ref, state_ref, blocks_scr, stage, state_scr, lists, sems, out_sems):
    load = pltpu.make_async_copy(blocks_ref, blocks_scr, sems.at[0])
    load.start()
    tiles, nnz = dest.shape[1:]
    each = nnz - 1
    rows = state_scr.shape[1]
    for t in range(tiles):
        state_scr[t] = jnp.transpose(seeds_ref[t].astype(jnp.float32)).astype(jnp.bfloat16)
    store = pltpu.make_async_copy(state_scr, state_ref, sems.at[1])
    store.start()
    for p in range(stage.shape[0]):
        lists[0, p] = 0
        lists[1, p] = tiles
    for t in range(tiles):
        for k in range(1, nnz):
            to = dest[0, t, k]
            peer = to // tiles
            lists[0, peer] = t * each + k - 1
            lists[1, peer] = to - peer * tiles
    for p in range(stage.shape[0]):
        stage[p, rows:] = jnp.full((SAYS, stage.shape[2]), lists[1, p], jnp.int32).astype(jnp.float32).astype(jnp.bfloat16)
    load.wait()
    wanted = Wanted(lambda p: lists[0, p], each)
    send_products(wanted, lambda n: blocks_scr[n + n // each + 1], state_scr, out_ref, stage, out_sems)
    store.wait()


def send_first(dest, seeds, blocks, peers):
    count, points = blocks.shape[:2]
    tiles, _, rows = seeds.shape
    return pl.pallas_call(
        first_body,
        out_shape=(
            jax.ShapeDtypeStruct((peers, rows + SAYS, points), jnp.bfloat16),
            jax.ShapeDtypeStruct((tiles, rows, points), jnp.bfloat16),
        ),
        in_specs=[SMEM, VMEM, HBM],
        out_specs=(HBM, HBM),
        scratch_shapes=[
            pltpu.VMEM(blocks.shape, jnp.bfloat16),
            pltpu.VMEM((peers, rows + SAYS, points), jnp.bfloat16),
            pltpu.VMEM((tiles, rows, points), jnp.bfloat16),
            pltpu.SMEM((2, peers), jnp.int32),
            pltpu.SemaphoreType.DMA((2,)),
            pltpu.SemaphoreType.DMA((peers // PART,)),
        ],
        compiler_params=SEND,
        cost_estimate=pl.CostEstimate(
            flops=2 * peers * points * points * rows, bytes_accessed=4 << 20, transcendentals=0
        ),
    )(dest, seeds, blocks)


def send_body(table, arrived_ref, local_ref, off_ref, out_ref, state_ref, stage, gathered, state_scr, store_sem, out_sems):
    each = off_ref.shape[0] // state_scr.shape[0]
    add_arrived(table, arrived_ref, gathered)
    for t in range(state_scr.shape[0]):
        state_scr[t] = (gathered[t] + local_ref[t]).astype(jnp.bfloat16)
    store = pltpu.make_async_copy(state_scr, state_ref, store_sem)
    store.start()
    wanted = Wanted(lambda p: table[WANTED, p], each)
    send_products(wanted, lambda n: off_ref[n], state_scr, out_ref, stage, out_sems)
    store.wait()


def send(table, arrived, local, off):
    peers = arrived.shape[0]
    tiles, rows, points = local.shape
    return pl.pallas_call(
        send_body,
        out_shape=(
            jax.ShapeDtypeStruct((peers, rows, points), jnp.bfloat16),
            jax.ShapeDtypeStruct((tiles, rows, points), jnp.bfloat16),
        ),
        in_specs=[SMEM] + SEND_SPECS,
        out_specs=(HBM, HBM),
        scratch_shapes=[
            pltpu.VMEM((peers, rows, points), jnp.bfloat16),
            pltpu.VMEM((tiles + 1, rows, points), jnp.float32),
            pltpu.VMEM((tiles, rows, points), jnp.bfloat16),
            pltpu.SemaphoreType.DMA,
            pltpu.SemaphoreType.DMA((peers // PART,)),
        ],
        compiler_params=SEND,
        cost_estimate=pl.CostEstimate(
            flops=2 * peers * points * points * rows, bytes_accessed=4 << 20, transcendentals=0
        ),
    )(table, arrived, local, off)


def keep_body(table, state_ref, diag_ref, off_ref, local_ref, total, sem):
    tiles = state_ref.shape[0]
    each = off_ref.shape[0] // tiles
    for t in range(tiles):
        total[t] = product(state_ref[t], diag_ref[t])
    for t in range(tiles):
        for k in range(each):
            home = table[HOME, t * each + k]
            total[home] = total[home] + product(state_ref[t], off_ref[t * each + k])
    store = pltpu.make_async_copy(total.at[pl.ds(0, tiles)], local_ref, sem)
    store.start()
    store.wait()


def keep(table, state, diag, off):
    tiles, rows, points = state.shape
    return pl.pallas_call(
        keep_body,
        out_shape=jax.ShapeDtypeStruct((tiles, rows, points), jnp.float32),
        in_specs=[SMEM, VMEM, VMEM, VMEM],
        out_specs=HBM,
        scratch_shapes=[pltpu.VMEM((tiles + 1, rows, points), jnp.float32), pltpu.SemaphoreType.DMA],
        compiler_params=KEEP,
        cost_estimate=pl.CostEstimate(
            flops=2 * (tiles + off.shape[0]) * points * points * rows, bytes_accessed=4 << 20, transcendentals=0
        ),
    )(table, state, diag, off)


def last_body(before, arrived_ref, local_ref, final_ref, edges_ref, gathered, local_scr, sem):
    load_local = pltpu.make_async_copy(local_ref, local_scr, sem)
    load_local.start()
    add_arrived(before, arrived_ref, gathered)
    load_local.wait()
    tiles = final_ref.shape[0]
    for t in range(tiles):
        final_ref[t] = (gathered[t] + local_scr[t]).astype(jnp.bfloat16)
    edges_ref[0] = final_ref[0]
    edges_ref[1] = final_ref[tiles - 1]


def last_sum(before, arrived, local):
    tiles, rows, points = local.shape
    return pl.pallas_call(
        last_body,
        out_shape=(
            jax.ShapeDtypeStruct((tiles, rows, points), jnp.bfloat16),
            jax.ShapeDtypeStruct((2, rows, points), jnp.bfloat16),
        ),
        in_specs=[SMEM, VMEM, HBM],
        out_specs=(VMEM, VMEM),
        scratch_shapes=[
            pltpu.VMEM((tiles + 1, rows, points), jnp.float32),
            pltpu.VMEM((tiles, rows, points), jnp.float32),
            pltpu.SemaphoreType.DMA,
        ],
        compiler_params=SMALL,
    )(before, arrived, local)


def stretch_tile(ndays, here, dy):
    rows, points = here.shape
    half = rows // 2
    lane = lax.broadcasted_iota(jnp.int32, (rows, points), 1)
    right = pltpu.roll(here, points - 1, 1)
    left = pltpu.roll(here, 1, 1)
    dx = jnp.where(lane == 0, right - here, jnp.where(lane == points - 1, here - left, (right - left) * 0.5))
    a, c = dx[:half], dx[half:]
    b, e = dy[:half], dy[half:]
    c11 = a * a + c * c
    c12 = a * b + c * e
    c22 = b * b + e * e
    gap = c11 - c22
    major = 0.5 * (c11 + c22 + jnp.sqrt(gap * gap + 4.0 * c12 * c12))
    lead = jnp.maximum(major, 1.0)
    det = a * e - b * c
    return jnp.log(lead) / (2.0 * ndays), det * det / lead


def inner_body(ndays, final_ref, ftle_ref, minor_ref):
    tiles, rows, points = final_ref.shape
    for t in range(1, tiles - 1):
        here = final_ref[t].astype(jnp.float32)
        dy = (final_ref[t + 1].astype(jnp.float32) - final_ref[t - 1].astype(jnp.float32)) * 0.5
        at = slice(t * points, (t + 1) * points)
        ftle_ref[:, at], minor_ref[:, at] = stretch_tile(ndays, here, dy)


def edge_body(ndays, place, final_ref, low_ref, high_ref, ftle_in, minor_in, ftle_ref, minor_ref, ftle_scr, minor_scr, sems):
    tiles, rows, points = final_ref.shape
    copies = []
    for i, t in enumerate((0, tiles - 1)):
        here = final_ref[t].astype(jnp.float32)
        below = (final_ref[t - 1] if t > 0 else low_ref[0]).astype(jnp.float32)
        above = (final_ref[t + 1] if t < tiles - 1 else high_ref[0]).astype(jnp.float32)
        one_sided = above - here if t == 0 else here - below
        dy = jnp.where(place[i] == 1, one_sided, (above - below) * 0.5)
        ftle_scr[i], minor_scr[i] = stretch_tile(ndays, here, dy)
        at = pl.ds(t * points, points)
        for n, (scr, ref) in enumerate(((ftle_scr, ftle_ref), (minor_scr, minor_ref))):
            copy = pltpu.make_async_copy(scr.at[i], ref.at[:, at], sems.at[2 * i + n])
            copy.start()
            copies.append(copy)
    for copy in copies:
        copy.wait()


def stretch_inner(final, ndays):
    tiles, rows, points = final.shape
    shape = jax.ShapeDtypeStruct((rows // 2, tiles * points), jnp.float32)
    return pl.pallas_call(
        functools.partial(inner_body, float(ndays)),
        out_shape=(shape, shape),
        in_specs=[VMEM],
        out_specs=(VMEM, VMEM),
        compiler_params=SMALL,
        cost_estimate=pl.CostEstimate(flops=40 * rows * tiles * points, bytes_accessed=2 << 20, transcendentals=0),
    )(final)


def stretch_edges(place, final, low, high, inner, ndays):
    tiles, rows, points = final.shape
    shape = jax.ShapeDtypeStruct((rows // 2, tiles * points), jnp.float32)
    scr = pltpu.VMEM((2, rows // 2, points), jnp.float32)
    return pl.pallas_call(
        functools.partial(edge_body, float(ndays)),
        out_shape=(shape, shape),
        in_specs=[SMEM, VMEM, VMEM, VMEM, HBM, HBM],
        out_specs=(HBM, HBM),
        scratch_shapes=[scr, scr, pltpu.SemaphoreType.DMA((4,))],
        input_output_aliases={4: 0, 5: 1},
        compiler_params=SMALL,
    )(place, final, low, high, *inner)


def own_rows(dest, me, tiles, peers, nnz):
    off = dest[:, 1:].reshape(tiles * (nnz - 1))
    peer = jnp.arange(peers, dtype=jnp.int32)
    order = jnp.arange(tiles * (nnz - 1), dtype=jnp.int32)
    wanted = jnp.max(jnp.where(off[None, :] // tiles == peer[:, None], order, 0), axis=1)
    home = jnp.where(off // tiles == me, off % tiles, tiles)
    return wanted, home


def body(seeds, blocks, dest_tiles):
    tiles, nnz, points = blocks.shape[1:4]
    width = seeds.shape[2]
    ndays, peers = lax.axis_size("day"), lax.axis_size("tile")
    me = lax.axis_index("tile")
    seeds = seeds.reshape(tiles, points, width)
    whole = blocks.reshape(tiles * nnz, points, points)
    diag, off = blocks[0, :, 0], blocks[0, :, 1:].reshape(tiles * (nnz - 1), points, points)
    onward = functools.partial(lax.ppermute, axis_name="day", perm=shifted(ndays, -1))

    for step in range(ndays):
        if step == 0:
            out, state = send_first(dest_tiles, seeds, whole, peers)
            dest, state = lax.optimization_barrier((dest_tiles[0], state))
            rows = own_rows(dest, me, tiles, peers, nnz)
            table = jnp.stack([*rows, jnp.zeros_like(rows[0])])
        else:
            out, state = send(table, arrived, local, off)
        arrived = lax.all_to_all(out, "tile", split_axis=0, concat_axis=0, tiled=True)
        local = keep(table, state, diag, off)
        table = onward(table)
        if step == 0:
            own = lax.broadcasted_iota(jnp.int32, (peers,), 0) == me
            landed = jnp.where(own, tiles, arrived[:, width, 0].astype(jnp.int32))
            table = jnp.concatenate([table[:2], landed[None]], axis=0)
        if step < ndays - 1:
            diag, off = onward(diag), onward(off)
    final, edges = last_sum(table, arrived, local)
    low = lax.ppermute(edges[1:], "tile", [(i, i + 1) for i in range(peers - 1)])
    high = lax.ppermute(edges[:1], "tile", [(i + 1, i) for i in range(peers - 1)])
    place = jnp.stack([me == 0, me == peers - 1]).astype(jnp.int32)
    inner = stretch_inner(final, ndays)
    ftle, minor = stretch_edges(place, final, low, high, inner, ndays)
    return ftle[None], minor[None]


def solution(mesh):
    in_specs = (P("day", "tile", None), P("day", "tile", None, None, None), P("day", "tile", None))
    out_specs = (P("day", None, "tile"), P("day", None, "tile"))
    return jax.shard_map(body, mesh=mesh, in_specs=in_specs, out_specs=out_specs, check_vma=False)
```

```python
import functools

import jax
import jax.numpy as jnp
from jax import lax
from jax.experimental import pallas as pl
from jax.experimental.pallas import tpu as pltpu
from jax.sharding import PartitionSpec as P

VMEM = pl.BlockSpec(memory_space=pltpu.VMEM)
SMEM = pl.BlockSpec(memory_space=pltpu.SMEM)
HBM = pl.BlockSpec(memory_space=pltpu.HBM)
SEND = pltpu.CompilerParams(vmem_limit_bytes=24 * 1024 * 1024)
KEEP = pltpu.CompilerParams(vmem_limit_bytes=24 * 1024 * 1024)
SMALL = pltpu.CompilerParams(vmem_limit_bytes=16 * 1024 * 1024)
PART = 4
SAYS = 16
WANTED, HOME, LANDED = range(3)


def shifted(n, by):
    return [(i, (i + by) % n) for i in range(n)]


def product(v, block):
    return lax.dot_general(v, block, (((1,), (1,)), ((), ())), preferred_element_type=jnp.float32)


def send_products(wanted, off_ref, state_ref, out_ref, stage, out_sems):
    rows, each = state_ref.shape[1], off_ref.shape[1]
    copies = []
    for p in range(stage.shape[0]):
        number = wanted(p)
        stage[p, :rows] = product(state_ref[lax.div(number, each)], off_ref[lax.div(number, each), lax.rem(number, each)]).astype(jnp.bfloat16)
        if p % PART == PART - 1:
            part = pl.ds(p + 1 - PART, PART)
            copy = pltpu.make_async_copy(stage.at[part], out_ref.at[part], out_sems.at[p // PART])
            copy.start()
            copies.append(copy)
    for copy in copies:
        copy.wait()


def add_arrived(table, arrived_ref, gathered):
    gathered[...] = jnp.zeros_like(gathered)
    rows = gathered.shape[1]
    for p in range(arrived_ref.shape[0]):
        home = table[LANDED, p]
        gathered[home] = gathered[home] + arrived_ref[p, :rows].astype(jnp.float32)


def off_copy(blocks_ref, off_scr, sem):
    return pltpu.make_async_copy(blocks_ref.at[:, pl.ds(1, off_scr.shape[1])], off_scr, sem)


def first_body(dest, seeds_ref, blocks_ref, out_ref, state_ref, off_scr, stage, state_scr, lists, sems, out_sems):
    load = off_copy(blocks_ref, off_scr, sems.at[0])
    load.start()
    tiles, nnz = dest.shape[1:]
    each = nnz - 1
    rows = state_scr.shape[1]
    for t in range(tiles):
        state_scr[t] = jnp.transpose(seeds_ref[t].astype(jnp.float32)).astype(jnp.bfloat16)
    store = pltpu.make_async_copy(state_scr, state_ref, sems.at[1])
    store.start()
    for p in range(stage.shape[0]):
        lists[0, p] = 0
        lists[1, p] = tiles
    for t in range(tiles):
        for k in range(1, nnz):
            to = dest[0, t, k]
            peer = lax.div(to, tiles)
            lists[0, peer] = t * each + k - 1
            lists[1, peer] = to - peer * tiles
    for p in range(stage.shape[0]):
        stage[p, rows:] = jnp.full((SAYS, stage.shape[2]), lists[1, p], jnp.int32).astype(jnp.float32).astype(jnp.bfloat16)
    load.wait()
    send_products(lambda p: lists[0, p], off_scr, state_scr, out_ref, stage, out_sems)
    store.wait()


def send_first(dest, seeds, blocks, peers):
    tiles, nnz, points = blocks.shape[:3]
    rows = seeds.shape[2]
    return pl.pallas_call(
        first_body,
        out_shape=(
            pltpu.HBM((peers, rows + SAYS, points), jnp.bfloat16),
            pltpu.HBM((tiles, rows, points), jnp.bfloat16),
        ),
        in_specs=[SMEM, VMEM, HBM],
        out_specs=(HBM, HBM),
        scratch_shapes=[
            pltpu.VMEM((tiles, nnz - 1, points, points), jnp.bfloat16),
            pltpu.VMEM((peers, rows + SAYS, points), jnp.bfloat16),
            pltpu.VMEM((tiles, rows, points), jnp.bfloat16),
            pltpu.SMEM((2, peers), jnp.int32),
            pltpu.SemaphoreType.DMA((2,)),
            pltpu.SemaphoreType.DMA((peers // PART,)),
        ],
        compiler_params=SEND,
        cost_estimate=pl.CostEstimate(
            flops=2 * peers * points * points * rows, bytes_accessed=4 << 20, transcendentals=0
        ),
    )(dest, seeds, placed(blocks, pltpu.HBM))


def send_body(
    table, arrived_ref, local_ref, blocks_ref, out_ref, state_ref,
    stage, gathered, state_scr, local_scr, off_scr, sems, out_sems,
):
    load_local = pltpu.make_async_copy(local_ref, local_scr, sems.at[0])
    load = off_copy(blocks_ref, off_scr, sems.at[1])
    load_local.start()
    load.start()
    add_arrived(table, arrived_ref, gathered)
    load_local.wait()
    for t in range(state_scr.shape[0]):
        state_scr[t] = (gathered[t] + local_scr[t]).astype(jnp.bfloat16)
    store = pltpu.make_async_copy(state_scr, state_ref, sems.at[2])
    store.start()
    load.wait()
    send_products(lambda p: table[WANTED, p], off_scr, state_scr, out_ref, stage, out_sems)
    store.wait()


placed = pltpu.with_memory_space_constraint


def send(table, arrived, local, blocks):
    peers = arrived.shape[0]
    tiles, rows, points = local.shape
    nnz = blocks.shape[1]
    return pl.pallas_call(
        send_body,
        out_shape=(
            pltpu.HBM((peers, rows, points), jnp.bfloat16),
            pltpu.HBM((tiles, rows, points), jnp.bfloat16),
        ),
        in_specs=[SMEM, VMEM, HBM, HBM],
        out_specs=(HBM, HBM),
        scratch_shapes=[
            pltpu.VMEM((peers, rows, points), jnp.bfloat16),
            pltpu.VMEM((tiles + 1, rows, points), jnp.float32),
            pltpu.VMEM((tiles, rows, points), jnp.bfloat16),
            pltpu.VMEM(local.shape, jnp.float32),
            pltpu.VMEM((tiles, nnz - 1, points, points), jnp.bfloat16),
            pltpu.SemaphoreType.DMA((3,)),
            pltpu.SemaphoreType.DMA((peers // PART,)),
        ],
        compiler_params=SEND,
        cost_estimate=pl.CostEstimate(
            flops=2 * peers * points * points * rows, bytes_accessed=4 << 20, transcendentals=0
        ),
    )(table, placed(arrived, pltpu.VMEM), placed(local, pltpu.HBM), placed(blocks, pltpu.HBM))


def keep_body(table, state_ref, blocks_ref, local_ref, total, blocks_scr, sem):
    load = pltpu.make_async_copy(blocks_ref, blocks_scr, sem)
    load.start()
    load.wait()
    tiles, nnz = blocks_scr.shape[:2]
    for t in range(tiles):
        total[t] = product(state_ref[t], blocks_scr[t, 0])
    for t in range(tiles):
        for k in range(1, nnz):
            home = table[HOME, t * (nnz - 1) + k - 1]
            total[home] = total[home] + product(state_ref[t], blocks_scr[t, k])
    local_ref[...] = total[pl.ds(0, tiles)]


def keep(table, state, blocks):
    tiles, rows, points = state.shape
    return pl.pallas_call(
        keep_body,
        out_shape=pltpu.HBM((tiles, rows, points), jnp.float32),
        in_specs=[SMEM, VMEM, HBM],
        out_specs=VMEM,
        scratch_shapes=[
            pltpu.VMEM((tiles + 1, rows, points), jnp.float32),
            pltpu.VMEM(blocks.shape, jnp.bfloat16),
            pltpu.SemaphoreType.DMA,
        ],
        compiler_params=KEEP,
        cost_estimate=pl.CostEstimate(
            flops=2 * tiles * blocks.shape[1] * points * points * rows, bytes_accessed=4 << 20, transcendentals=0
        ),
    )(table, placed(state, pltpu.HBM), placed(blocks, pltpu.HBM))


def last_body(before, arrived_ref, local_ref, final_ref, edges_ref, gathered, local_scr, sem):
    load_local = pltpu.make_async_copy(local_ref, local_scr, sem)
    load_local.start()
    add_arrived(before, arrived_ref, gathered)
    load_local.wait()
    tiles = final_ref.shape[0]
    for t in range(tiles):
        final_ref[t] = (gathered[t] + local_scr[t]).astype(jnp.bfloat16)
    edges_ref[0] = final_ref[0]
    edges_ref[1] = final_ref[tiles - 1]


def last_sum(before, arrived, local):
    tiles, rows, points = local.shape
    return pl.pallas_call(
        last_body,
        out_shape=(
            jax.ShapeDtypeStruct((tiles, rows, points), jnp.bfloat16),
            jax.ShapeDtypeStruct((2, rows, points), jnp.bfloat16),
        ),
        in_specs=[SMEM, VMEM, HBM],
        out_specs=(VMEM, VMEM),
        scratch_shapes=[
            pltpu.VMEM((tiles + 1, rows, points), jnp.float32),
            pltpu.VMEM((tiles, rows, points), jnp.float32),
            pltpu.SemaphoreType.DMA,
        ],
        compiler_params=SMALL,
    )(before, arrived, local)


def stretch_tile(ndays, here, dy):
    rows, points = here.shape
    half = rows // 2
    lane = lax.broadcasted_iota(jnp.int32, (rows, points), 1)
    right = pltpu.roll(here, points - 1, 1)
    left = pltpu.roll(here, 1, 1)
    dx = jnp.where(lane == 0, right - here, jnp.where(lane == points - 1, here - left, (right - left) * 0.5))
    a, c = dx[:half], dx[half:]
    b, e = dy[:half], dy[half:]
    c11 = a * a + c * c
    c12 = a * b + c * e
    c22 = b * b + e * e
    gap = c11 - c22
    major = 0.5 * (c11 + c22 + jnp.sqrt(gap * gap + 4.0 * c12 * c12))
    lead = jnp.maximum(major, 1.0)
    det = a * e - b * c
    return jnp.log(lead) / (2.0 * ndays), det * det / lead


def inner_body(ndays, final_ref, ftle_ref, minor_ref):
    tiles, rows, points = final_ref.shape
    for t in range(1, tiles - 1):
        here = final_ref[t].astype(jnp.float32)
        dy = (final_ref[t + 1].astype(jnp.float32) - final_ref[t - 1].astype(jnp.float32)) * 0.5
        at = slice(t * points, (t + 1) * points)
        ftle_ref[:, at], minor_ref[:, at] = stretch_tile(ndays, here, dy)


def edge_body(ndays, place, final_ref, low_ref, high_ref, ftle_in, minor_in, ftle_ref, minor_ref, ftle_scr, minor_scr, sems):
    tiles, rows, points = final_ref.shape
    copies = []
    for i, t in enumerate((0, tiles - 1)):
        here = final_ref[t].astype(jnp.float32)
        below = (final_ref[t - 1] if t > 0 else low_ref[0]).astype(jnp.float32)
        above = (final_ref[t + 1] if t < tiles - 1 else high_ref[0]).astype(jnp.float32)
        one_sided = above - here if t == 0 else here - below
        dy = jnp.where(place[i] == 1, one_sided, (above - below) * 0.5)
        ftle_scr[i], minor_scr[i] = stretch_tile(ndays, here, dy)
        at = pl.ds(t * points, points)
        for n, (scr, ref) in enumerate(((ftle_scr, ftle_ref), (minor_scr, minor_ref))):
            copy = pltpu.make_async_copy(scr.at[i], ref.at[:, at], sems.at[2 * i + n])
            copy.start()
            copies.append(copy)
    for copy in copies:
        copy.wait()


def stretch_inner(final, ndays):
    tiles, rows, points = final.shape
    shape = jax.ShapeDtypeStruct((rows // 2, tiles * points), jnp.float32)
    return pl.pallas_call(
        functools.partial(inner_body, float(ndays)),
        out_shape=(shape, shape),
        in_specs=[VMEM],
        out_specs=(VMEM, VMEM),
        compiler_params=SMALL,
        cost_estimate=pl.CostEstimate(flops=40 * rows * tiles * points, bytes_accessed=2 << 20, transcendentals=0),
    )(final)


def stretch_edges(place, final, low, high, inner, ndays):
    tiles, rows, points = final.shape
    shape = jax.ShapeDtypeStruct((rows // 2, tiles * points), jnp.float32)
    scr = pltpu.VMEM((2, rows // 2, points), jnp.float32)
    return pl.pallas_call(
        functools.partial(edge_body, float(ndays)),
        out_shape=(shape, shape),
        in_specs=[SMEM, VMEM, VMEM, VMEM, HBM, HBM],
        out_specs=(HBM, HBM),
        scratch_shapes=[scr, scr, pltpu.SemaphoreType.DMA((4,))],
        input_output_aliases={4: 0, 5: 1},
        compiler_params=SMALL,
    )(place, final, low, high, *inner)


def own_rows(dest, me, tiles, peers, nnz):
    off = dest[:, 1:].reshape(tiles * (nnz - 1))
    peer = jnp.arange(peers, dtype=jnp.int32)
    order = jnp.arange(tiles * (nnz - 1), dtype=jnp.int32)
    wanted = jnp.max(jnp.where(off[None, :] // tiles == peer[:, None], order, 0), axis=1)
    home = jnp.where(off // tiles == me, off % tiles, tiles)
    return wanted, home


def body(seeds, blocks, dest_tiles):
    tiles, nnz, points = blocks.shape[1:4]
    width = seeds.shape[2]
    ndays, peers = lax.axis_size("day"), lax.axis_size("tile")
    me = lax.axis_index("tile")
    seeds = seeds.reshape(tiles, points, width)
    wblk = blocks[0]
    onward = functools.partial(lax.ppermute, axis_name="day", perm=shifted(ndays, -1))

    for step in range(ndays):
        if step == 0:
            out, state = send_first(dest_tiles, seeds, wblk, peers)
            dest, state = lax.optimization_barrier((dest_tiles[0], state))
            rows = own_rows(dest, me, tiles, peers, nnz)
            table = jnp.stack([*rows, jnp.zeros_like(rows[0])])
        else:
            out, state = send(table, arrived, local, wblk)
        arrived = lax.all_to_all(out, "tile", split_axis=0, concat_axis=0, tiled=True)
        local = keep(table, state, wblk)
        table = onward(table)
        if step == 0:
            own = lax.broadcasted_iota(jnp.int32, (peers,), 0) == me
            landed = jnp.where(own, tiles, arrived[:, width, 0].astype(jnp.int32))
            table = jnp.concatenate([table[:2], landed[None]], axis=0)
        if step < ndays - 1:
            wblk = onward(wblk)
    final, edges = last_sum(table, arrived, placed(local, pltpu.HBM))
    low = lax.ppermute(edges[1:], "tile", [(i, i + 1) for i in range(peers - 1)])
    high = lax.ppermute(edges[:1], "tile", [(i + 1, i) for i in range(peers - 1)])
    place = jnp.stack([me == 0, me == peers - 1]).astype(jnp.int32)
    inner = stretch_inner(final, ndays)
    ftle, minor = stretch_edges(place, final, low, high, inner, ndays)
    return ftle[None], minor[None]


def solution(mesh):
    in_specs = (P("day", "tile", None), P("day", "tile", None, None, None), P("day", "tile", None))
    out_specs = (P("day", None, "tile"), P("day", None, "tile"))
    return jax.shard_map(body, mesh=mesh, in_specs=in_specs, out_specs=out_specs, check_vma=False)
```

```python
import functools

import jax
import jax.numpy as jnp
from jax import lax
from jax.experimental import pallas as pl
from jax.experimental.pallas import tpu as pltpu
from jax.sharding import PartitionSpec as P

VMEM = pl.BlockSpec(memory_space=pltpu.VMEM)
SMEM = pl.BlockSpec(memory_space=pltpu.SMEM)
HBM = pl.BlockSpec(memory_space=pltpu.HBM)
SEND = pltpu.CompilerParams(vmem_limit_bytes=24 * 1024 * 1024)
KEEP = pltpu.CompilerParams(vmem_limit_bytes=24 * 1024 * 1024)
SMALL = pltpu.CompilerParams(vmem_limit_bytes=16 * 1024 * 1024)
PART = 4
SAYS = 16
WANTED, HOME, LANDED = range(3)


def shifted(n, by):
    return [(i, (i + by) % n) for i in range(n)]


def product(v, block):
    return lax.dot_general(v, block, (((1,), (1,)), ((), ())), preferred_element_type=jnp.float32)


def send_products(wanted, off_ref, state_ref, out_ref, stage, out_sems):
    rows, each = state_ref.shape[1], off_ref.shape[1]
    copies = []
    for p in range(stage.shape[0]):
        number = wanted(p)
        stage[p, :rows] = product(state_ref[lax.div(number, each)], off_ref[lax.div(number, each), lax.rem(number, each)]).astype(jnp.bfloat16)
        if p % PART == PART - 1:
            part = pl.ds(p + 1 - PART, PART)
            copy = pltpu.make_async_copy(stage.at[part], out_ref.at[part], out_sems.at[p // PART])
            copy.start()
            copies.append(copy)
    for copy in copies:
        copy.wait()


def add_arrived(table, arrived_ref, gathered):
    gathered[...] = jnp.zeros_like(gathered)
    rows = gathered.shape[1]
    for p in range(arrived_ref.shape[0]):
        home = table[LANDED, p]
        gathered[home] = gathered[home] + arrived_ref[p, :rows].astype(jnp.float32)


def off_copy(blocks_ref, off_scr, sem):
    return pltpu.make_async_copy(blocks_ref.at[:, pl.ds(1, off_scr.shape[1])], off_scr, sem)


def first_body(
    dest, seeds_ref, blocks_ref, out_ref, state_ref, seeds_scr, off_scr, stage, state_scr, lists, sems, out_sems, in_sems
):
    nnz, tiles = dest.shape
    each = nnz - 1
    rows = state_scr.shape[1]
    parts = [pl.ds(t, PART) for t in range(0, tiles, PART)]
    seeding = [pltpu.make_async_copy(seeds_ref.at[p], seeds_scr.at[p], in_sems.at[n]) for n, p in enumerate(parts)]
    load = off_copy(blocks_ref, off_scr, sems.at[0])
    for copy in [*seeding, load]:
        copy.start()
    for t in range(tiles):
        if t % PART == 0:
            seeding[t // PART].wait()
        state_scr[t] = jnp.transpose(seeds_scr[t].astype(jnp.float32)).astype(jnp.bfloat16)
    store = pltpu.make_async_copy(state_scr, state_ref, sems.at[1])
    store.start()
    for p in range(stage.shape[0]):
        lists[0, p] = 0
        lists[1, p] = tiles
    for t in range(tiles):
        for k in range(1, nnz):
            to = dest[k, t]
            peer = lax.div(to, tiles)
            lists[0, peer] = t * each + k - 1
            lists[1, peer] = to - peer * tiles
    for p in range(stage.shape[0]):
        stage[p, rows:] = jnp.full((SAYS, stage.shape[2]), lists[1, p], jnp.int32).astype(jnp.float32).astype(jnp.bfloat16)
    load.wait()
    send_products(lambda p: lists[0, p], off_scr, state_scr, out_ref, stage, out_sems)
    store.wait()


def send_first(dest, seeds, blocks, peers):
    tiles, nnz, points = blocks.shape[:3]
    rows = seeds.shape[2]
    return pl.pallas_call(
        first_body,
        out_shape=(
            pltpu.HBM((peers, rows + SAYS, points), jnp.bfloat16),
            pltpu.HBM((tiles, rows, points), jnp.bfloat16),
        ),
        in_specs=[SMEM, HBM, HBM],
        out_specs=(HBM, HBM),
        scratch_shapes=[
            pltpu.VMEM(seeds.shape, jnp.bfloat16),
            pltpu.VMEM((tiles, nnz - 1, points, points), jnp.bfloat16),
            pltpu.VMEM((peers, rows + SAYS, points), jnp.bfloat16),
            pltpu.VMEM((tiles, rows, points), jnp.bfloat16),
            pltpu.SMEM((2, peers), jnp.int32),
            pltpu.SemaphoreType.DMA((2,)),
            pltpu.SemaphoreType.DMA((peers // PART,)),
            pltpu.SemaphoreType.DMA((tiles // PART,)),
        ],
        compiler_params=SEND,
        cost_estimate=pl.CostEstimate(
            flops=2 * peers * points * points * rows, bytes_accessed=4 << 20, transcendentals=0
        ),
    )(dest, placed(seeds, pltpu.HBM), placed(blocks, pltpu.HBM))


def fetch_body(blocks_ref, off_ref, sem):
    load = off_copy(blocks_ref, off_ref, sem)
    load.start()
    load.wait()


def fetch(blocks):
    tiles, nnz, points = blocks.shape[:3]
    return pl.pallas_call(
        fetch_body,
        out_shape=pltpu.VMEM((tiles, nnz - 1, points, points), jnp.bfloat16),
        in_specs=[HBM],
        out_specs=VMEM,
        scratch_shapes=[pltpu.SemaphoreType.DMA],
        compiler_params=SMALL,
        cost_estimate=pl.CostEstimate(flops=0, bytes_accessed=2 << 20, transcendentals=0),
    )(placed(blocks, pltpu.HBM))


def send_body(
    table, arrived_ref, local_ref, off_ref, out_ref, state_ref, stage, gathered, state_scr, store_sem, out_sems,
):
    add_arrived(table, arrived_ref, gathered)
    for t in range(state_scr.shape[0]):
        state_scr[t] = (gathered[t] + local_ref[t]).astype(jnp.bfloat16)
    store = pltpu.make_async_copy(state_scr, state_ref, store_sem)
    store.start()
    send_products(lambda p: table[WANTED, p], off_ref, state_scr, out_ref, stage, out_sems)
    store.wait()


placed = pltpu.with_memory_space_constraint


def send(table, arrived, local, off):
    peers = arrived.shape[0]
    tiles, rows, points = local.shape
    return pl.pallas_call(
        send_body,
        out_shape=(
            pltpu.HBM((peers, rows, points), jnp.bfloat16),
            pltpu.HBM((tiles, rows, points), jnp.bfloat16),
        ),
        in_specs=[SMEM, VMEM, VMEM, VMEM],
        out_specs=(HBM, HBM),
        scratch_shapes=[
            pltpu.VMEM((peers, rows, points), jnp.bfloat16),
            pltpu.VMEM((tiles + 1, rows, points), jnp.float32),
            pltpu.VMEM((tiles, rows, points), jnp.bfloat16),
            pltpu.SemaphoreType.DMA,
            pltpu.SemaphoreType.DMA((peers // PART,)),
        ],
        compiler_params=SEND,
        cost_estimate=pl.CostEstimate(
            flops=2 * peers * points * points * rows, bytes_accessed=4 << 20, transcendentals=0
        ),
    )(table, placed(arrived, pltpu.VMEM), placed(local, pltpu.VMEM), placed(off, pltpu.VMEM))


def keep_body(table, state_ref, blocks_ref, local_ref, total, blocks_scr, sem):
    load = pltpu.make_async_copy(blocks_ref, blocks_scr, sem)
    load.start()
    load.wait()
    tiles, nnz = blocks_scr.shape[:2]
    for t in range(tiles):
        total[t] = product(state_ref[t], blocks_scr[t, 0])
    for t in range(tiles):
        for k in range(1, nnz):
            home = table[HOME, t * (nnz - 1) + k - 1]
            total[home] = total[home] + product(state_ref[t], blocks_scr[t, k])
    local_ref[...] = total[pl.ds(0, tiles)]


def keep(table, state, blocks):
    tiles, rows, points = state.shape
    return pl.pallas_call(
        keep_body,
        out_shape=pltpu.VMEM((tiles, rows, points), jnp.float32),
        in_specs=[SMEM, VMEM, HBM],
        out_specs=VMEM,
        scratch_shapes=[
            pltpu.VMEM((tiles + 1, rows, points), jnp.float32),
            pltpu.VMEM(blocks.shape, jnp.bfloat16),
            pltpu.SemaphoreType.DMA,
        ],
        compiler_params=KEEP,
        cost_estimate=pl.CostEstimate(
            flops=2 * tiles * blocks.shape[1] * points * points * rows, bytes_accessed=4 << 20, transcendentals=0
        ),
    )(table, placed(state, pltpu.HBM), placed(blocks, pltpu.HBM))


def last_body(before, arrived_ref, local_ref, final_ref, low_ref, high_ref, gathered):
    add_arrived(before, arrived_ref, gathered)
    tiles = final_ref.shape[0]
    for t in range(tiles):
        final_ref[t] = (gathered[t] + local_ref[t]).astype(jnp.bfloat16)
    low_ref[0] = final_ref[0]
    high_ref[0] = final_ref[tiles - 1]


def last_sum(before, arrived, local):
    tiles, rows, points = local.shape
    return pl.pallas_call(
        last_body,
        out_shape=(
            jax.ShapeDtypeStruct((tiles, rows, points), jnp.bfloat16),
            jax.ShapeDtypeStruct((1, rows, points), jnp.bfloat16),
            jax.ShapeDtypeStruct((1, rows, points), jnp.bfloat16),
        ),
        in_specs=[SMEM, VMEM, VMEM],
        out_specs=(VMEM, VMEM, VMEM),
        scratch_shapes=[
            pltpu.VMEM((tiles + 1, rows, points), jnp.float32),
        ],
        compiler_params=SMALL,
    )(before, placed(arrived, pltpu.VMEM), placed(local, pltpu.VMEM))


def stretch_tile(ndays, here, dy):
    rows, points = here.shape
    half = rows // 2
    lane = lax.broadcasted_iota(jnp.int32, (rows, points), 1)
    right = pltpu.roll(here, points - 1, 1)
    left = pltpu.roll(here, 1, 1)
    dx = jnp.where(lane == 0, right - here, jnp.where(lane == points - 1, here - left, (right - left) * 0.5))
    a, c = dx[:half], dx[half:]
    b, e = dy[:half], dy[half:]
    c11 = a * a + c * c
    c12 = a * b + c * e
    c22 = b * b + e * e
    gap = c11 - c22
    major = 0.5 * (c11 + c22 + jnp.sqrt(gap * gap + 4.0 * c12 * c12))
    lead = jnp.maximum(major, 1.0)
    det = a * e - b * c
    return jnp.log(lead) / (2.0 * ndays), det * det / lead


def inner_body(ndays, final_ref, ftle_ref, minor_ref):
    tiles, rows, points = final_ref.shape
    for t in range(1, tiles - 1):
        here = final_ref[t].astype(jnp.float32)
        dy = (final_ref[t + 1].astype(jnp.float32) - final_ref[t - 1].astype(jnp.float32)) * 0.5
        at = slice(t * points, (t + 1) * points)
        ftle_ref[:, at], minor_ref[:, at] = stretch_tile(ndays, here, dy)


def edge_body(ndays, place, final_ref, low_ref, high_ref, ftle_in, minor_in, ftle_ref, minor_ref, ftle_scr, minor_scr, sems):
    tiles, rows, points = final_ref.shape
    copies = []
    for i, t in enumerate((0, tiles - 1)):
        here = final_ref[t].astype(jnp.float32)
        below = (final_ref[t - 1] if t > 0 else low_ref[0]).astype(jnp.float32)
        above = (final_ref[t + 1] if t < tiles - 1 else high_ref[0]).astype(jnp.float32)
        one_sided = above - here if t == 0 else here - below
        dy = jnp.where(place[i] == 1, one_sided, (above - below) * 0.5)
        ftle_scr[i], minor_scr[i] = stretch_tile(ndays, here, dy)
        at = pl.ds(t * points, points)
        for n, (scr, ref) in enumerate(((ftle_scr, ftle_ref), (minor_scr, minor_ref))):
            copy = pltpu.make_async_copy(scr.at[i], ref.at[:, at], sems.at[2 * i + n])
            copy.start()
            copies.append(copy)
    for copy in copies:
        copy.wait()


def stretch_inner(final, ndays):
    tiles, rows, points = final.shape
    shape = jax.ShapeDtypeStruct((rows // 2, tiles * points), jnp.float32)
    return pl.pallas_call(
        functools.partial(inner_body, float(ndays)),
        out_shape=(shape, shape),
        in_specs=[VMEM],
        out_specs=(VMEM, VMEM),
        compiler_params=SMALL,
        cost_estimate=pl.CostEstimate(flops=40 * rows * tiles * points, bytes_accessed=2 << 20, transcendentals=0),
    )(final)


def stretch_edges(place, final, low, high, inner, ndays):
    tiles, rows, points = final.shape
    shape = jax.ShapeDtypeStruct((rows // 2, tiles * points), jnp.float32)
    scr = pltpu.VMEM((2, rows // 2, points), jnp.float32)
    return pl.pallas_call(
        functools.partial(edge_body, float(ndays)),
        out_shape=(shape, shape),
        in_specs=[SMEM, VMEM, VMEM, VMEM, HBM, HBM],
        out_specs=(HBM, HBM),
        scratch_shapes=[scr, scr, pltpu.SemaphoreType.DMA((4,))],
        input_output_aliases={4: 0, 5: 1},
        compiler_params=SMALL,
    )(place, final, low, high, *inner)


def own_rows(dest, me, tiles, peers, nnz):
    off = dest[:, 1:].reshape(tiles * (nnz - 1))
    peer = jnp.arange(peers, dtype=jnp.int32)
    order = jnp.arange(tiles * (nnz - 1), dtype=jnp.int32)
    wanted = jnp.max(jnp.where(off[None, :] // tiles == peer[:, None], order, 0), axis=1)
    home = jnp.where(off // tiles == me, off % tiles, tiles)
    return wanted, home


def body(seeds, blocks, dest_tiles):
    tiles, nnz, points = blocks.shape[1:4]
    width = seeds.shape[2]
    ndays, peers = lax.axis_size("day"), lax.axis_size("tile")
    me = lax.axis_index("tile")
    seeds = seeds.reshape(tiles, points, width)
    wblk = blocks[0]
    onward = functools.partial(lax.ppermute, axis_name="day", perm=shifted(ndays, -1))

    for step in range(ndays):
        if step == 0:
            out, state = send_first(dest_tiles.transpose(2, 0, 1).reshape(nnz, tiles), seeds, wblk, peers)
            dest, state = lax.optimization_barrier((dest_tiles[0], state))
            rows = own_rows(dest, me, tiles, peers, nnz)
            table = jnp.stack([*rows, jnp.zeros_like(rows[0])])
        else:
            out, state = send(table, arrived, local, off)
        arrived = lax.all_to_all(out, "tile", split_axis=0, concat_axis=0, tiled=True)
        local = keep(table, state, wblk)
        table = onward(table)
        if step == 0:
            own = lax.broadcasted_iota(jnp.int32, (peers,), 0) == me
            landed = jnp.where(own, tiles, arrived[:, width, 0].astype(jnp.int32))
            table = jnp.concatenate([table[:2], landed[None]], axis=0)
        if step < ndays - 1:
            wblk = onward(wblk)
            off = fetch(wblk)
    final, lowest, highest = last_sum(table, arrived, local)
    low = lax.ppermute(highest, "tile", [(i, i + 1) for i in range(peers - 1)])
    high = lax.ppermute(lowest, "tile", [(i + 1, i) for i in range(peers - 1)])
    place = jnp.stack([me == 0, me == peers - 1]).astype(jnp.int32)
    inner = stretch_inner(final, ndays)
    ftle, minor = stretch_edges(place, final, low, high, inner, ndays)
    return ftle[None], minor[None]


def solution(mesh):
    in_specs = (P("day", "tile", None), P("day", "tile", None, None, None), P("day", "tile", None))
    out_specs = (P("day", None, "tile"), P("day", None, "tile"))
    return jax.shard_map(body, mesh=mesh, in_specs=in_specs, out_specs=out_specs, check_vma=False)
```

```python
import functools

import jax
import jax.numpy as jnp
from jax import lax
from jax.experimental import pallas as pl
from jax.experimental.pallas import tpu as pltpu
from jax.sharding import PartitionSpec as P

VMEM = pl.BlockSpec(memory_space=pltpu.VMEM)
SMEM = pl.BlockSpec(memory_space=pltpu.SMEM)
HBM = pl.BlockSpec(memory_space=pltpu.HBM)
SEND = pltpu.CompilerParams(vmem_limit_bytes=24 * 1024 * 1024)
KEEP = pltpu.CompilerParams(vmem_limit_bytes=24 * 1024 * 1024)
SMALL = pltpu.CompilerParams(vmem_limit_bytes=16 * 1024 * 1024)
PART = 4
SAYS = 16
WANTED, HOME, LANDED = range(3)


def shifted(n, by):
    return [(i, (i + by) % n) for i in range(n)]


def product(v, block):
    return lax.dot_general(v, block, (((1,), (1,)), ((), ())), preferred_element_type=jnp.float32)


def send_products(wanted, off_ref, state_ref, out_ref, stage, out_sems):
    rows, each = state_ref.shape[1], off_ref.shape[1]
    copies = []
    for p in range(stage.shape[0]):
        number = wanted(p)
        stage[p, :rows] = product(state_ref[lax.div(number, each)], off_ref[lax.div(number, each), lax.rem(number, each)]).astype(jnp.bfloat16)
        if p % PART == PART - 1:
            part = pl.ds(p + 1 - PART, PART)
            copy = pltpu.make_async_copy(stage.at[part], out_ref.at[part], out_sems.at[p // PART])
            copy.start()
            copies.append(copy)
    for copy in copies:
        copy.wait()


def add_arrived(table, arrived_ref, gathered):
    gathered[...] = jnp.zeros_like(gathered)
    rows = gathered.shape[1]
    for p in range(arrived_ref.shape[0]):
        home = table[LANDED, p]
        gathered[home] = gathered[home] + arrived_ref[p, :rows].astype(jnp.float32)


def off_copy(blocks_ref, off_scr, sem):
    return pltpu.make_async_copy(blocks_ref.at[:, pl.ds(1, off_scr.shape[1])], off_scr, sem)


def first_body(
    dest, seeds_ref, blocks_ref, out_ref, state_ref, seeds_scr, off_scr, stage, state_scr, lists, sems, out_sems, in_sems
):
    nnz, tiles = dest.shape
    each = nnz - 1
    rows = state_scr.shape[1]
    parts = [pl.ds(t, PART) for t in range(0, tiles, PART)]
    seeding = [pltpu.make_async_copy(seeds_ref.at[p], seeds_scr.at[p], in_sems.at[n]) for n, p in enumerate(parts)]
    load = off_copy(blocks_ref, off_scr, sems.at[0])
    for copy in [*seeding, load]:
        copy.start()
    for t in range(tiles):
        if t % PART == 0:
            seeding[t // PART].wait()
        state_scr[t] = jnp.transpose(seeds_scr[t].astype(jnp.float32)).astype(jnp.bfloat16)
    store = pltpu.make_async_copy(state_scr, state_ref, sems.at[1])
    store.start()
    for p in range(stage.shape[0]):
        lists[0, p] = 0
        lists[1, p] = tiles
    for t in range(tiles):
        for k in range(1, nnz):
            to = dest[k, t]
            peer = lax.div(to, tiles)
            lists[0, peer] = t * each + k - 1
            lists[1, peer] = to - peer * tiles
    for p in range(stage.shape[0]):
        stage[p, rows:] = jnp.full((SAYS, stage.shape[2]), lists[1, p], jnp.int32).astype(jnp.float32).astype(jnp.bfloat16)
    load.wait()
    send_products(lambda p: lists[0, p], off_scr, state_scr, out_ref, stage, out_sems)
    store.wait()


def send_first(dest, seeds, blocks, peers):
    tiles, nnz, points = blocks.shape[:3]
    rows = seeds.shape[2]
    return pl.pallas_call(
        first_body,
        out_shape=(
            pltpu.HBM((peers, rows + SAYS, points), jnp.bfloat16),
            pltpu.HBM((tiles, rows, points), jnp.bfloat16),
        ),
        in_specs=[SMEM, HBM, HBM],
        out_specs=(HBM, HBM),
        scratch_shapes=[
            pltpu.VMEM(seeds.shape, jnp.bfloat16),
            pltpu.VMEM((tiles, nnz - 1, points, points), jnp.bfloat16),
            pltpu.VMEM((peers, rows + SAYS, points), jnp.bfloat16),
            pltpu.VMEM((tiles, rows, points), jnp.bfloat16),
            pltpu.SMEM((2, peers), jnp.int32),
            pltpu.SemaphoreType.DMA((2,)),
            pltpu.SemaphoreType.DMA((peers // PART,)),
            pltpu.SemaphoreType.DMA((tiles // PART,)),
        ],
        compiler_params=SEND,
        cost_estimate=pl.CostEstimate(
            flops=2 * peers * points * points * rows, bytes_accessed=4 << 20, transcendentals=0
        ),
    )(dest, placed(seeds, pltpu.HBM), placed(blocks, pltpu.HBM))


def fetch_body(blocks_ref, off_ref, sem):
    load = off_copy(blocks_ref, off_ref, sem)
    load.start()
    load.wait()


def fetch(blocks):
    tiles, nnz, points = blocks.shape[:3]
    return pl.pallas_call(
        fetch_body,
        out_shape=pltpu.VMEM((tiles, nnz - 1, points, points), jnp.bfloat16),
        in_specs=[HBM],
        out_specs=VMEM,
        scratch_shapes=[pltpu.SemaphoreType.DMA],
        compiler_params=SMALL,
        cost_estimate=pl.CostEstimate(flops=0, bytes_accessed=2 << 20, transcendentals=0),
    )(placed(blocks, pltpu.HBM))


def send_body(
    table, arrived_ref, local_ref, off_ref, out_ref, state_ref, stage, gathered, state_scr, store_sem, out_sems,
):
    add_arrived(table, arrived_ref, gathered)
    for t in range(state_scr.shape[0]):
        state_scr[t] = (gathered[t] + local_ref[t]).astype(jnp.bfloat16)
    store = pltpu.make_async_copy(state_scr, state_ref, store_sem)
    store.start()
    send_products(lambda p: table[WANTED, p], off_ref, state_scr, out_ref, stage, out_sems)
    store.wait()


placed = pltpu.with_memory_space_constraint


def send(table, arrived, local, off):
    peers = arrived.shape[0]
    tiles, rows, points = local.shape
    return pl.pallas_call(
        send_body,
        out_shape=(
            pltpu.HBM((peers, rows, points), jnp.bfloat16),
            pltpu.HBM((tiles, rows, points), jnp.bfloat16),
        ),
        in_specs=[SMEM, VMEM, VMEM, VMEM],
        out_specs=(HBM, HBM),
        scratch_shapes=[
            pltpu.VMEM((peers, rows, points), jnp.bfloat16),
            pltpu.VMEM((tiles + 1, rows, points), jnp.float32),
            pltpu.VMEM((tiles, rows, points), jnp.bfloat16),
            pltpu.SemaphoreType.DMA,
            pltpu.SemaphoreType.DMA((peers // PART,)),
        ],
        compiler_params=SEND,
        cost_estimate=pl.CostEstimate(
            flops=2 * peers * points * points * rows, bytes_accessed=4 << 20, transcendentals=0
        ),
    )(table, placed(arrived, pltpu.VMEM), placed(local, pltpu.VMEM), placed(off, pltpu.VMEM))


def keep_body(table, state_ref, blocks_ref, local_ref, total, blocks_scr, sem):
    load = pltpu.make_async_copy(blocks_ref, blocks_scr, sem)
    load.start()
    load.wait()
    tiles, nnz = blocks_scr.shape[:2]
    for t in range(tiles):
        total[t] = product(state_ref[t], blocks_scr[t, 0])
    for t in range(tiles):
        for k in range(1, nnz):
            home = table[HOME, t * (nnz - 1) + k - 1]
            total[home] = total[home] + product(state_ref[t], blocks_scr[t, k])
    local_ref[...] = total[pl.ds(0, tiles)]


def keep(table, state, blocks):
    tiles, rows, points = state.shape
    return pl.pallas_call(
        keep_body,
        out_shape=pltpu.VMEM((tiles, rows, points), jnp.float32),
        in_specs=[SMEM, VMEM, HBM],
        out_specs=VMEM,
        scratch_shapes=[
            pltpu.VMEM((tiles + 1, rows, points), jnp.float32),
            pltpu.VMEM(blocks.shape, jnp.bfloat16),
            pltpu.SemaphoreType.DMA,
        ],
        compiler_params=KEEP,
        cost_estimate=pl.CostEstimate(
            flops=2 * tiles * blocks.shape[1] * points * points * rows, bytes_accessed=4 << 20, transcendentals=0
        ),
    )(table, placed(state, pltpu.HBM), placed(blocks, pltpu.HBM))


def last_body(before, arrived_ref, local_ref, final_ref, low_ref, high_ref, gathered):
    add_arrived(before, arrived_ref, gathered)
    tiles = final_ref.shape[0]
    for t in range(tiles):
        final_ref[t] = (gathered[t] + local_ref[t]).astype(jnp.bfloat16)
    low_ref[0] = final_ref[0]
    high_ref[0] = final_ref[tiles - 1]


def last_sum(before, arrived, local):
    tiles, rows, points = local.shape
    return pl.pallas_call(
        last_body,
        out_shape=(
            jax.ShapeDtypeStruct((tiles, rows, points), jnp.bfloat16),
            jax.ShapeDtypeStruct((1, rows, points), jnp.bfloat16),
            jax.ShapeDtypeStruct((1, rows, points), jnp.bfloat16),
        ),
        in_specs=[SMEM, VMEM, VMEM],
        out_specs=(VMEM, VMEM, VMEM),
        scratch_shapes=[
            pltpu.VMEM((tiles + 1, rows, points), jnp.float32),
        ],
        compiler_params=SMALL,
    )(before, placed(arrived, pltpu.VMEM), placed(local, pltpu.VMEM))


def stretch_tile(ndays, here, dy):
    rows, points = here.shape
    half = rows // 2
    lane = lax.broadcasted_iota(jnp.int32, (rows, points), 1)
    right = pltpu.roll(here, points - 1, 1)
    left = pltpu.roll(here, 1, 1)
    dx = jnp.where(lane == 0, right - here, jnp.where(lane == points - 1, here - left, (right - left) * 0.5))
    a, c = dx[:half], dx[half:]
    b, e = dy[:half], dy[half:]
    c11 = a * a + c * c
    c12 = a * b + c * e
    c22 = b * b + e * e
    gap = c11 - c22
    major = 0.5 * (c11 + c22 + jnp.sqrt(gap * gap + 4.0 * c12 * c12))
    lead = jnp.maximum(major, 1.0)
    det = a * e - b * c
    return jnp.log(lead) / (2.0 * ndays), det * det / lead


def inner_body(ndays, final_ref, ftle_ref, minor_ref):
    tiles, rows, points = final_ref.shape
    for t in range(1, tiles - 1):
        here = final_ref[t].astype(jnp.float32)
        dy = (final_ref[t + 1].astype(jnp.float32) - final_ref[t - 1].astype(jnp.float32)) * 0.5
        at = slice(t * points, (t + 1) * points)
        ftle_ref[:, at], minor_ref[:, at] = stretch_tile(ndays, here, dy)


def edge_body(ndays, place, final_ref, low_ref, high_ref, ftle_in, minor_in, ftle_ref, minor_ref, ftle_scr, minor_scr, sems):
    tiles, rows, points = final_ref.shape
    copies = []
    for i, t in enumerate((0, tiles - 1)):
        here = final_ref[t].astype(jnp.float32)
        below = (final_ref[t - 1] if t > 0 else low_ref[0]).astype(jnp.float32)
        above = (final_ref[t + 1] if t < tiles - 1 else high_ref[0]).astype(jnp.float32)
        one_sided = above - here if t == 0 else here - below
        dy = jnp.where(place[i] == 1, one_sided, (above - below) * 0.5)
        ftle_scr[i], minor_scr[i] = stretch_tile(ndays, here, dy)
        at = pl.ds(t * points, points)
        for n, (scr, ref) in enumerate(((ftle_scr, ftle_ref), (minor_scr, minor_ref))):
            copy = pltpu.make_async_copy(scr.at[i], ref.at[:, at], sems.at[2 * i + n])
            copy.start()
            copies.append(copy)
    for copy in copies:
        copy.wait()


def stretch_inner(final, ndays):
    tiles, rows, points = final.shape
    shape = jax.ShapeDtypeStruct((rows // 2, tiles * points), jnp.float32)
    return pl.pallas_call(
        functools.partial(inner_body, float(ndays)),
        out_shape=(shape, shape),
        in_specs=[VMEM],
        out_specs=(VMEM, VMEM),
        compiler_params=SMALL,
        cost_estimate=pl.CostEstimate(flops=40 * rows * tiles * points, bytes_accessed=2 << 20, transcendentals=0),
    )(final)


def stretch_edges(place, final, low, high, inner, ndays):
    tiles, rows, points = final.shape
    shape = jax.ShapeDtypeStruct((rows // 2, tiles * points), jnp.float32)
    scr = pltpu.VMEM((2, rows // 2, points), jnp.float32)
    return pl.pallas_call(
        functools.partial(edge_body, float(ndays)),
        out_shape=(shape, shape),
        in_specs=[SMEM, VMEM, VMEM, VMEM, HBM, HBM],
        out_specs=(HBM, HBM),
        scratch_shapes=[scr, scr, pltpu.SemaphoreType.DMA((4,))],
        input_output_aliases={4: 0, 5: 1},
        compiler_params=SMALL,
    )(place, final, low, high, *inner)


def own_rows(dest, me, tiles, peers, nnz):
    off = dest[:, 1:].reshape(tiles * (nnz - 1))
    peer = jnp.arange(peers, dtype=jnp.int32)
    order = jnp.arange(tiles * (nnz - 1), dtype=jnp.int32)
    wanted = jnp.max(jnp.where(off[None, :] // tiles == peer[:, None], order, 0), axis=1)
    home = jnp.where(off // tiles == me, off % tiles, tiles)
    return wanted, home


def body(seeds, blocks, dest_tiles):
    tiles, nnz, points = blocks.shape[1:4]
    width = seeds.shape[2]
    ndays, peers = lax.axis_size("day"), lax.axis_size("tile")
    me = lax.axis_index("tile")
    seeds = seeds.reshape(tiles, points, width)
    wblk = blocks[0]
    onward = functools.partial(lax.ppermute, axis_name="day", perm=shifted(ndays, -1))

    for step in range(ndays):
        if step == 0:
            out, state = send_first(dest_tiles.transpose(2, 0, 1).reshape(nnz, tiles), seeds, wblk, peers)
            dest, state = lax.optimization_barrier((dest_tiles[0], state))
            rows = own_rows(dest, me, tiles, peers, nnz)
            table = jnp.stack([*rows, jnp.zeros_like(rows[0])])
        else:
            out, state = send(table, arrived, local, off)
        arrived = lax.all_to_all(out, "tile", split_axis=0, concat_axis=0, tiled=True)
        local = keep(table, state, wblk)
        table = onward(table)
        if step == 0:
            own = lax.broadcasted_iota(jnp.int32, (peers,), 0) == me
            landed = jnp.where(own, tiles, arrived[:, width, 0].astype(jnp.int32))
            table = jnp.concatenate([table[:2], landed[None]], axis=0)
        if step < ndays - 1:
            wblk = onward(wblk)
            wblk, local = lax.optimization_barrier((wblk, local))
            off = fetch(wblk)
    final, lowest, highest = last_sum(table, arrived, local)
    low = lax.ppermute(highest, "tile", [(i, i + 1) for i in range(peers - 1)])
    high = lax.ppermute(lowest, "tile", [(i + 1, i) for i in range(peers - 1)])
    place = jnp.stack([me == 0, me == peers - 1]).astype(jnp.int32)
    inner = stretch_inner(final, ndays)
    ftle, minor = stretch_edges(place, final, low, high, inner, ndays)
    return ftle[None], minor[None]


def solution(mesh):
    in_specs = (P("day", "tile", None), P("day", "tile", None, None, None), P("day", "tile", None))
    out_specs = (P("day", None, "tile"), P("day", None, "tile"))
    return jax.shard_map(body, mesh=mesh, in_specs=in_specs, out_specs=out_specs, check_vma=False)
```

```python
import functools

import jax
import jax.numpy as jnp
from jax import lax
from jax.experimental import pallas as pl
from jax.experimental.pallas import tpu as pltpu
from jax.sharding import PartitionSpec as P

VMEM = pl.BlockSpec(memory_space=pltpu.VMEM)
SMEM = pl.BlockSpec(memory_space=pltpu.SMEM)
HBM = pl.BlockSpec(memory_space=pltpu.HBM)
SEND = pltpu.CompilerParams(vmem_limit_bytes=24 * 1024 * 1024)
KEEP = pltpu.CompilerParams(vmem_limit_bytes=24 * 1024 * 1024)
SMALL = pltpu.CompilerParams(vmem_limit_bytes=16 * 1024 * 1024)
PART = 4
SAYS = 16
WANTED, HOME, LANDED = range(3)


def shifted(n, by):
    return [(i, (i + by) % n) for i in range(n)]


def product(v, block):
    return lax.dot_general(v, block, (((1,), (1,)), ((), ())), preferred_element_type=jnp.float32)


def send_products(wanted, off_ref, state_ref, out_ref, stage, out_sems):
    rows, each = state_ref.shape[1], off_ref.shape[1]
    copies = []
    for p in range(stage.shape[0]):
        number = wanted(p)
        stage[p, :rows] = product(state_ref[lax.div(number, each)], off_ref[lax.div(number, each), lax.rem(number, each)]).astype(jnp.bfloat16)
        if p % PART == PART - 1:
            part = pl.ds(p + 1 - PART, PART)
            copy = pltpu.make_async_copy(stage.at[part], out_ref.at[part], out_sems.at[p // PART])
            copy.start()
            copies.append(copy)
    for copy in copies:
        copy.wait()


def add_arrived(table, arrived_ref, gathered):
    gathered[...] = jnp.zeros_like(gathered)
    rows = gathered.shape[1]
    for p in range(arrived_ref.shape[0]):
        home = table[LANDED, p]
        gathered[home] = gathered[home] + arrived_ref[p, :rows].astype(jnp.float32)


def off_copy(blocks_ref, off_scr, sem):
    return pltpu.make_async_copy(blocks_ref.at[:, pl.ds(1, off_scr.shape[1])], off_scr, sem)


def first_body(
    dest, seeds_ref, blocks_ref, out_ref, state_ref, seeds_scr, off_scr, stage, state_scr, lists, sems, out_sems, in_sems
):
    nnz, _, tiles = dest.shape
    each = nnz - 1
    rows = state_scr.shape[1]
    parts = [pl.ds(t, PART) for t in range(0, tiles, PART)]
    seeding = [pltpu.make_async_copy(seeds_ref.at[p], seeds_scr.at[p], in_sems.at[n]) for n, p in enumerate(parts)]
    load = off_copy(blocks_ref, off_scr, sems.at[0])
    for copy in [*seeding, load]:
        copy.start()
    for t in range(tiles):
        if t % PART == 0:
            seeding[t // PART].wait()
        state_scr[t] = jnp.transpose(seeds_scr[t])
    store = pltpu.make_async_copy(state_scr, state_ref, sems.at[1])
    store.start()
    for p in range(stage.shape[0]):
        lists[0, p] = 0
        lists[1, p] = tiles
    for t in range(tiles):
        for k in range(1, nnz):
            to = dest[k, 0, t]
            peer = lax.div(to, tiles)
            lists[0, peer] = t * each + k - 1
            lists[1, peer] = to - peer * tiles
    for p in range(stage.shape[0]):
        stage[p, rows:] = jnp.full((SAYS, stage.shape[2]), lists[1, p], jnp.int32).astype(jnp.float32).astype(jnp.bfloat16)
    load.wait()
    send_products(lambda p: lists[0, p], off_scr, state_scr, out_ref, stage, out_sems)
    store.wait()


def send_first(dest, seeds, blocks, peers):
    tiles, nnz, points = blocks.shape[:3]
    rows = seeds.shape[2]
    return pl.pallas_call(
        first_body,
        out_shape=(
            pltpu.HBM((peers, rows + SAYS, points), jnp.bfloat16),
            pltpu.HBM((tiles, rows, points), jnp.bfloat16),
        ),
        in_specs=[SMEM, HBM, HBM],
        out_specs=(HBM, HBM),
        scratch_shapes=[
            pltpu.VMEM(seeds.shape, jnp.bfloat16),
            pltpu.VMEM((tiles, nnz - 1, points, points), jnp.bfloat16),
            pltpu.VMEM((peers, rows + SAYS, points), jnp.bfloat16),
            pltpu.VMEM((tiles, rows, points), jnp.bfloat16),
            pltpu.SMEM((2, peers), jnp.int32),
            pltpu.SemaphoreType.DMA((2,)),
            pltpu.SemaphoreType.DMA((peers // PART,)),
            pltpu.SemaphoreType.DMA((tiles // PART,)),
        ],
        compiler_params=SEND,
        cost_estimate=pl.CostEstimate(
            flops=2 * peers * points * points * rows, bytes_accessed=4 << 20, transcendentals=0
        ),
    )(placed(dest, pltpu.HBM), placed(seeds, pltpu.HBM), placed(blocks, pltpu.HBM))


def fetch_body(blocks_ref, table_ref, off_ref, read_ref, sems):
    loads = [off_copy(blocks_ref, off_ref, sems.at[0]), pltpu.make_async_copy(table_ref, read_ref, sems.at[1])]
    for load in loads:
        load.start()
    for load in loads:
        load.wait()


def fetch(blocks, table):
    tiles, nnz, points = blocks.shape[:3]
    return pl.pallas_call(
        fetch_body,
        out_shape=(
            pltpu.VMEM((tiles, nnz - 1, points, points), jnp.bfloat16),
            pltpu.SMEM(table.shape, jnp.int32),
        ),
        in_specs=[HBM, HBM],
        out_specs=(VMEM, SMEM),
        scratch_shapes=[pltpu.SemaphoreType.DMA((2,))],
        compiler_params=SMALL,
        cost_estimate=pl.CostEstimate(flops=0, bytes_accessed=2 << 20, transcendentals=0),
    )(placed(blocks, pltpu.HBM), placed(table, pltpu.HBM))


def hold_body(table_ref, read_ref, sem):
    load = pltpu.make_async_copy(table_ref, read_ref, sem)
    load.start()
    load.wait()


def hold(table):
    return pl.pallas_call(
        hold_body,
        out_shape=pltpu.SMEM(table.shape, jnp.int32),
        in_specs=[HBM],
        out_specs=SMEM,
        scratch_shapes=[pltpu.SemaphoreType.DMA],
        compiler_params=SMALL,
        cost_estimate=pl.CostEstimate(flops=0, bytes_accessed=1 << 10, transcendentals=0),
    )(placed(table, pltpu.HBM))


def send_body(
    table, arrived_ref, local_ref, off_ref, out_ref, state_ref, stage, gathered, state_scr, store_sem, out_sems,
):
    add_arrived(table, arrived_ref, gathered)
    for t in range(state_scr.shape[0]):
        state_scr[t] = (gathered[t] + local_ref[t]).astype(jnp.bfloat16)
    store = pltpu.make_async_copy(state_scr, state_ref, store_sem)
    store.start()
    send_products(lambda p: table[WANTED, p], off_ref, state_scr, out_ref, stage, out_sems)
    store.wait()


placed = pltpu.with_memory_space_constraint


def send(table, arrived, local, off, ready):
    peers = arrived.shape[0]
    tiles, rows, points = local.shape
    return pl.pallas_call(
        send_body,
        out_shape=(
            pltpu.HBM((peers, rows, points), jnp.bfloat16),
            pltpu.HBM((tiles, rows, points), jnp.bfloat16),
        ),
        in_specs=[SMEM, VMEM, VMEM, VMEM],
        out_specs=(HBM, HBM),
        scratch_shapes=[
            pltpu.VMEM((peers, rows, points), jnp.bfloat16),
            pltpu.VMEM((tiles + 1, rows, points), jnp.float32),
            pltpu.VMEM((tiles, rows, points), jnp.bfloat16),
            pltpu.SemaphoreType.DMA,
            pltpu.SemaphoreType.DMA((peers // PART,)),
        ],
        compiler_params=SEND,
        cost_estimate=pl.CostEstimate(
            flops=2 * peers * points * points * rows, bytes_accessed=4 << 20, transcendentals=0
        ),
    )(placed(table, pltpu.SMEM) if ready else table, placed(arrived, pltpu.VMEM), placed(local, pltpu.VMEM), placed(off, pltpu.VMEM))


def keep_body(table, state_ref, blocks_ref, local_ref, total, blocks_scr, sem):
    load = pltpu.make_async_copy(blocks_ref, blocks_scr, sem)
    load.start()
    load.wait()
    tiles, nnz = blocks_scr.shape[:2]
    for t in range(tiles):
        total[t] = product(state_ref[t], blocks_scr[t, 0])
    for t in range(tiles):
        for k in range(1, nnz):
            home = table[HOME, t * (nnz - 1) + k - 1]
            total[home] = total[home] + product(state_ref[t], blocks_scr[t, k])
    local_ref[...] = total[pl.ds(0, tiles)]


def keep(table, state, blocks):
    tiles, rows, points = state.shape
    return pl.pallas_call(
        keep_body,
        out_shape=pltpu.VMEM((tiles, rows, points), jnp.float32),
        in_specs=[SMEM, VMEM, HBM],
        out_specs=VMEM,
        scratch_shapes=[
            pltpu.VMEM((tiles + 1, rows, points), jnp.float32),
            pltpu.VMEM(blocks.shape, jnp.bfloat16),
            pltpu.SemaphoreType.DMA,
        ],
        compiler_params=KEEP,
        cost_estimate=pl.CostEstimate(
            flops=2 * tiles * blocks.shape[1] * points * points * rows, bytes_accessed=4 << 20, transcendentals=0
        ),
    )(table, placed(state, pltpu.HBM), placed(blocks, pltpu.HBM))


def last_body(before, arrived_ref, local_ref, final_ref, low_ref, high_ref, gathered):
    add_arrived(before, arrived_ref, gathered)
    tiles = final_ref.shape[0]
    for t in range(tiles):
        final_ref[t] = (gathered[t] + local_ref[t]).astype(jnp.bfloat16)
    low_ref[0] = final_ref[0]
    high_ref[0] = final_ref[tiles - 1]


def last_sum(before, arrived, local):
    tiles, rows, points = local.shape
    return pl.pallas_call(
        last_body,
        out_shape=(
            jax.ShapeDtypeStruct((tiles, rows, points), jnp.bfloat16),
            jax.ShapeDtypeStruct((1, rows, points), jnp.bfloat16),
            jax.ShapeDtypeStruct((1, rows, points), jnp.bfloat16),
        ),
        in_specs=[SMEM, VMEM, VMEM],
        out_specs=(VMEM, VMEM, VMEM),
        scratch_shapes=[
            pltpu.VMEM((tiles + 1, rows, points), jnp.float32),
        ],
        compiler_params=SMALL,
    )(placed(before, pltpu.SMEM), placed(arrived, pltpu.VMEM), placed(local, pltpu.VMEM))


def stretch_tile(ndays, here, dy):
    rows, points = here.shape
    half = rows // 2
    lane = lax.broadcasted_iota(jnp.int32, (rows, points), 1)
    right = pltpu.roll(here, points - 1, 1)
    left = pltpu.roll(here, 1, 1)
    dx = jnp.where(lane == 0, right - here, jnp.where(lane == points - 1, here - left, (right - left) * 0.5))
    a, c = dx[:half], dx[half:]
    b, e = dy[:half], dy[half:]
    c11 = a * a + c * c
    c12 = a * b + c * e
    c22 = b * b + e * e
    gap = c11 - c22
    major = 0.5 * (c11 + c22 + jnp.sqrt(gap * gap + 4.0 * c12 * c12))
    lead = jnp.maximum(major, 1.0)
    det = a * e - b * c
    return jnp.log(lead) / (2.0 * ndays), det * det / lead


def inner_body(ndays, final_ref, ftle_ref, minor_ref):
    tiles, rows, points = final_ref.shape
    for t in range(1, tiles - 1):
        here = final_ref[t].astype(jnp.float32)
        dy = (final_ref[t + 1].astype(jnp.float32) - final_ref[t - 1].astype(jnp.float32)) * 0.5
        at = slice(t * points, (t + 1) * points)
        ftle_ref[:, at], minor_ref[:, at] = stretch_tile(ndays, here, dy)


def edge_body(ndays, final_ref, low_ref, high_ref, ftle_in, minor_in, ftle_ref, minor_ref, ftle_scr, minor_scr, sems):
    tiles, rows, points = final_ref.shape
    copies = []
    for i, t in enumerate((0, tiles - 1)):
        here = final_ref[t].astype(jnp.float32)
        below = (final_ref[t - 1] if t > 0 else low_ref[0]).astype(jnp.float32)
        above = (final_ref[t + 1] if t < tiles - 1 else high_ref[0]).astype(jnp.float32)
        one_sided = above - here if t == 0 else here - below
        at_end = lax.axis_index("tile") == (0 if t == 0 else lax.axis_size("tile") - 1)
        dy = jnp.where(at_end, one_sided, (above - below) * 0.5)
        ftle_scr[i], minor_scr[i] = stretch_tile(ndays, here, dy)
        at = pl.ds(t * points, points)
        for n, (scr, ref) in enumerate(((ftle_scr, ftle_ref), (minor_scr, minor_ref))):
            copy = pltpu.make_async_copy(scr.at[i], ref.at[:, at], sems.at[2 * i + n])
            copy.start()
            copies.append(copy)
    for copy in copies:
        copy.wait()


def stretch_inner(final, ndays):
    tiles, rows, points = final.shape
    shape = jax.ShapeDtypeStruct((rows // 2, tiles * points), jnp.float32)
    return pl.pallas_call(
        functools.partial(inner_body, float(ndays)),
        out_shape=(shape, shape),
        in_specs=[VMEM],
        out_specs=(VMEM, VMEM),
        compiler_params=SMALL,
        cost_estimate=pl.CostEstimate(flops=40 * rows * tiles * points, bytes_accessed=2 << 20, transcendentals=0),
    )(final)


def stretch_edges(final, low, high, inner, ndays):
    tiles, rows, points = final.shape
    shape = jax.ShapeDtypeStruct((rows // 2, tiles * points), jnp.float32)
    scr = pltpu.VMEM((2, rows // 2, points), jnp.float32)
    return pl.pallas_call(
        functools.partial(edge_body, float(ndays)),
        out_shape=(shape, shape),
        in_specs=[VMEM, VMEM, VMEM, HBM, HBM],
        out_specs=(HBM, HBM),
        scratch_shapes=[scr, scr, pltpu.SemaphoreType.DMA((4,))],
        input_output_aliases={3: 0, 4: 1},
        compiler_params=SMALL,
    )(final, low, high, *inner)


def own_rows(dest, me, tiles, peers, nnz):
    off = dest[:, 1:].reshape(tiles * (nnz - 1))
    peer = jnp.arange(peers, dtype=jnp.int32)
    order = jnp.arange(tiles * (nnz - 1), dtype=jnp.int32)
    wanted = jnp.max(jnp.where(off[None, :] // tiles == peer[:, None], order, 0), axis=1)
    home = jnp.where(off // tiles == me, off % tiles, tiles)
    return wanted, home


def body(seeds, blocks, dest_tiles):
    tiles, nnz, points = blocks.shape[1:4]
    width = seeds.shape[2]
    ndays, peers = lax.axis_size("day"), lax.axis_size("tile")
    me = lax.axis_index("tile")
    seeds = seeds.reshape(tiles, points, width)
    wblk = blocks[0]
    onward = functools.partial(lax.ppermute, axis_name="day", perm=shifted(ndays, -1))

    for step in range(ndays):
        if step == 0:
            out, state = send_first(dest_tiles.transpose(2, 0, 1), seeds, wblk, peers)
            dest, state = lax.optimization_barrier((dest_tiles[0], state))
            rows = own_rows(dest, me, tiles, peers, nnz)
            table = jnp.stack([*rows, jnp.zeros_like(rows[0])])
        else:
            out, state = send(table if step == 1 else quick, arrived, local, off, step > 1)
        arrived = lax.all_to_all(out, "tile", split_axis=0, concat_axis=0, tiled=True)
        local = keep(table, state, wblk)
        given = table = onward(table)
        if step == 0:
            own = lax.broadcasted_iota(jnp.int32, (peers,), 0) == me
            landed = jnp.where(own, tiles, arrived[:, width, 0].astype(jnp.int32))
            table = jnp.concatenate([table[:2], landed[None]], axis=0)
        if step < ndays - 1:
            wblk = onward(wblk)
            wblk, local = lax.optimization_barrier((wblk, local))
            off, quick = fetch(wblk, table if step else given)
    final, lowest, highest = last_sum(hold(table), arrived, local)
    low = lax.ppermute(highest, "tile", [(i, i + 1) for i in range(peers - 1)])
    high = lax.ppermute(lowest, "tile", [(i + 1, i) for i in range(peers - 1)])
    inner = stretch_inner(final, ndays)
    ftle, minor = stretch_edges(final, low, high, inner, ndays)
    return ftle[None], minor[None]


def solution(mesh):
    in_specs = (P("day", "tile", None), P("day", "tile", None, None, None), P("day", "tile", None))
    out_specs = (P("day", None, "tile"), P("day", None, "tile"))
    return jax.shard_map(body, mesh=mesh, in_specs=in_specs, out_specs=out_specs, check_vma=False)
```

```python
import functools

import jax
import jax.numpy as jnp
from jax import lax
from jax.experimental import pallas as pl
from jax.experimental.pallas import tpu as pltpu
from jax.sharding import PartitionSpec as P

VMEM = pl.BlockSpec(memory_space=pltpu.VMEM)
SMEM = pl.BlockSpec(memory_space=pltpu.SMEM)
HBM = pl.BlockSpec(memory_space=pltpu.HBM)
SEND = pltpu.CompilerParams(vmem_limit_bytes=24 * 1024 * 1024)
KEEP = pltpu.CompilerParams(vmem_limit_bytes=24 * 1024 * 1024)
SMALL = pltpu.CompilerParams(vmem_limit_bytes=16 * 1024 * 1024)
PART = 4
SAYS = 16
WANTED, HOME, LANDED = range(3)


def shifted(n, by):
    return [(i, (i + by) % n) for i in range(n)]


def product(v, block):
    return lax.dot_general(v, block, (((1,), (1,)), ((), ())), preferred_element_type=jnp.float32)


def send_products(wanted, off_ref, state_ref, out_ref, stage, out_sems):
    rows, each = state_ref.shape[1], off_ref.shape[1]
    copies = []
    for p in range(stage.shape[0]):
        number = wanted(p)
        stage[p, :rows] = product(state_ref[lax.div(number, each)], off_ref[lax.div(number, each), lax.rem(number, each)]).astype(jnp.bfloat16)
        if p % PART == PART - 1:
            part = pl.ds(p + 1 - PART, PART)
            copy = pltpu.make_async_copy(stage.at[part], out_ref.at[part], out_sems.at[p // PART])
            copy.start()
            copies.append(copy)
    for copy in copies:
        copy.wait()


def add_arrived(landed, arrived_ref, gathered):
    gathered[...] = jnp.zeros_like(gathered)
    rows = gathered.shape[1]
    for p in range(arrived_ref.shape[0]):
        home = landed(p)
        gathered[home] = gathered[home] + arrived_ref[p, :rows].astype(jnp.float32)


def off_copy(blocks_ref, off_scr, sem):
    return pltpu.make_async_copy(blocks_ref.at[:, pl.ds(1, off_scr.shape[1])], off_scr, sem)


def first_body(
    dest_ref, seeds_ref, blocks_ref, out_ref, state_ref, seeds_scr, off_scr, stage, state_scr, dest, lists, sems, out_sems, in_sems
):
    nnz, _, tiles = dest.shape
    read = pltpu.make_async_copy(dest_ref, dest, sems.at[2])
    read.start()
    each = nnz - 1
    rows = state_scr.shape[1]
    parts = [pl.ds(t, PART) for t in range(0, tiles, PART)]
    seeding = [pltpu.make_async_copy(seeds_ref.at[p], seeds_scr.at[p], in_sems.at[n]) for n, p in enumerate(parts)]
    load = off_copy(blocks_ref, off_scr, sems.at[0])
    for copy in [*seeding, load]:
        copy.start()
    for t in range(tiles):
        if t % PART == 0:
            seeding[t // PART].wait()
        state_scr[t] = jnp.transpose(seeds_scr[t])
    store = pltpu.make_async_copy(state_scr, state_ref, sems.at[1])
    store.start()
    read.wait()
    for p in range(stage.shape[0]):
        lists[0, p] = 0
        lists[1, p] = tiles
    for t in range(tiles):
        for k in range(1, nnz):
            to = dest[k, 0, t]
            peer = lax.div(to, tiles)
            lists[0, peer] = t * each + k - 1
            lists[1, peer] = to - peer * tiles
    for p in range(stage.shape[0]):
        stage[p, rows:] = jnp.full((SAYS, stage.shape[2]), lists[1, p], jnp.int32).astype(jnp.float32).astype(jnp.bfloat16)
    load.wait()
    send_products(lambda p: lists[0, p], off_scr, state_scr, out_ref, stage, out_sems)
    store.wait()


def send_first(dest, seeds, blocks, peers):
    tiles, nnz, points = blocks.shape[:3]
    rows = seeds.shape[2]
    return pl.pallas_call(
        first_body,
        out_shape=(
            pltpu.HBM((peers, rows + SAYS, points), jnp.bfloat16),
            pltpu.HBM((tiles, rows, points), jnp.bfloat16),
        ),
        in_specs=[HBM, HBM, HBM],
        out_specs=(HBM, HBM),
        scratch_shapes=[
            pltpu.VMEM(seeds.shape, jnp.bfloat16),
            pltpu.VMEM((tiles, nnz - 1, points, points), jnp.bfloat16),
            pltpu.VMEM((peers, rows + SAYS, points), jnp.bfloat16),
            pltpu.VMEM((tiles, rows, points), jnp.bfloat16),
            pltpu.SMEM(dest.shape, jnp.int32),
            pltpu.SMEM((2, peers), jnp.int32),
            pltpu.SemaphoreType.DMA((3,)),
            pltpu.SemaphoreType.DMA((peers // PART,)),
            pltpu.SemaphoreType.DMA((tiles // PART,)),
        ],
        compiler_params=SEND,
        cost_estimate=pl.CostEstimate(
            flops=2 * peers * points * points * rows, bytes_accessed=4 << 20, transcendentals=0
        ),
    )(placed(dest, pltpu.HBM), placed(seeds, pltpu.HBM), placed(blocks, pltpu.HBM))


def fetch_body(blocks_ref, table_ref, off_ref, read_ref, sems):
    loads = [off_copy(blocks_ref, off_ref, sems.at[0]), pltpu.make_async_copy(table_ref, read_ref, sems.at[1])]
    for load in loads:
        load.start()
    for load in loads:
        load.wait()


def fetch(blocks, table):
    tiles, nnz, points = blocks.shape[:3]
    return pl.pallas_call(
        fetch_body,
        out_shape=(
            pltpu.VMEM((tiles, nnz - 1, points, points), jnp.bfloat16),
            pltpu.SMEM(table.shape, jnp.int32),
        ),
        in_specs=[HBM, HBM],
        out_specs=(VMEM, SMEM),
        scratch_shapes=[pltpu.SemaphoreType.DMA((2,))],
        compiler_params=SMALL,
        cost_estimate=pl.CostEstimate(flops=0, bytes_accessed=2 << 20, transcendentals=0),
    )(placed(blocks, pltpu.HBM), placed(table, pltpu.HBM))


def hold_body(table_ref, read_ref, sem):
    load = pltpu.make_async_copy(table_ref, read_ref, sem)
    load.start()
    load.wait()


def hold(table):
    return pl.pallas_call(
        hold_body,
        out_shape=pltpu.SMEM(table.shape, jnp.int32),
        in_specs=[HBM],
        out_specs=SMEM,
        scratch_shapes=[pltpu.SemaphoreType.DMA],
        compiler_params=SMALL,
        cost_estimate=pl.CostEstimate(flops=0, bytes_accessed=1 << 10, transcendentals=0),
    )(placed(table, pltpu.HBM))


def send_body(
    table, arrived_ref, local_ref, off_ref, out_ref, state_ref, stage, gathered, state_scr, store_sem, out_sems, *told,
):
    landed = lambda p: table[LANDED, p]
    if told:
        said, read, sem = told
        said[...] = arrived_ref[:, state_scr.shape[1], :].astype(jnp.float32).astype(jnp.int32)
        copy = pltpu.make_async_copy(said, read, sem)
        copy.start()
        copy.wait()
        me = lax.axis_index("tile")
        landed = lambda p: jnp.where(me == p, state_scr.shape[0], read[p, 0])
    add_arrived(landed, arrived_ref, gathered)
    for t in range(state_scr.shape[0]):
        state_scr[t] = (gathered[t] + local_ref[t]).astype(jnp.bfloat16)
    store = pltpu.make_async_copy(state_scr, state_ref, store_sem)
    store.start()
    send_products(lambda p: table[WANTED, p], off_ref, state_scr, out_ref, stage, out_sems)
    store.wait()


placed = pltpu.with_memory_space_constraint


def send(table, arrived, local, off):
    peers = arrived.shape[0]
    tiles, rows, points = local.shape
    told = []
    if arrived.shape[1] > rows:
        told = [pltpu.VMEM((peers, points), jnp.int32), pltpu.SMEM((peers, points), jnp.int32), pltpu.SemaphoreType.DMA]
    return pl.pallas_call(
        send_body,
        out_shape=(
            pltpu.HBM((peers, rows, points), jnp.bfloat16),
            pltpu.HBM((tiles, rows, points), jnp.bfloat16),
        ),
        in_specs=[SMEM, VMEM, VMEM, VMEM],
        out_specs=(HBM, HBM),
        scratch_shapes=[
            pltpu.VMEM((peers, rows, points), jnp.bfloat16),
            pltpu.VMEM((tiles + 1, rows, points), jnp.float32),
            pltpu.VMEM((tiles, rows, points), jnp.bfloat16),
            pltpu.SemaphoreType.DMA,
            pltpu.SemaphoreType.DMA((peers // PART,)),
            *told,
        ],
        compiler_params=SEND,
        cost_estimate=pl.CostEstimate(
            flops=2 * peers * points * points * rows, bytes_accessed=4 << 20, transcendentals=0
        ),
    )(placed(table, pltpu.SMEM), placed(arrived, pltpu.VMEM), placed(local, pltpu.VMEM), placed(off, pltpu.VMEM))


def keep_body(table, state_ref, blocks_ref, local_ref, total, blocks_scr, sem):
    load = pltpu.make_async_copy(blocks_ref, blocks_scr, sem)
    load.start()
    load.wait()
    tiles, nnz = blocks_scr.shape[:2]
    for t in range(tiles):
        total[t] = product(state_ref[t], blocks_scr[t, 0])
    for t in range(tiles):
        for k in range(1, nnz):
            home = table[HOME, t * (nnz - 1) + k - 1]
            total[home] = total[home] + product(state_ref[t], blocks_scr[t, k])
    local_ref[...] = total[pl.ds(0, tiles)]


def keep(table, state, blocks):
    tiles, rows, points = state.shape
    return pl.pallas_call(
        keep_body,
        out_shape=pltpu.VMEM((tiles, rows, points), jnp.float32),
        in_specs=[SMEM, VMEM, HBM],
        out_specs=VMEM,
        scratch_shapes=[
            pltpu.VMEM((tiles + 1, rows, points), jnp.float32),
            pltpu.VMEM(blocks.shape, jnp.bfloat16),
            pltpu.SemaphoreType.DMA,
        ],
        compiler_params=KEEP,
        cost_estimate=pl.CostEstimate(
            flops=2 * tiles * blocks.shape[1] * points * points * rows, bytes_accessed=4 << 20, transcendentals=0
        ),
    )(table, placed(state, pltpu.HBM), placed(blocks, pltpu.HBM))


def last_body(before, arrived_ref, local_ref, final_ref, low_ref, high_ref, gathered):
    add_arrived(lambda p: before[LANDED, p], arrived_ref, gathered)
    tiles = final_ref.shape[0]
    for t in range(tiles):
        final_ref[t] = (gathered[t] + local_ref[t]).astype(jnp.bfloat16)
    low_ref[0] = final_ref[0]
    high_ref[0] = final_ref[tiles - 1]


def last_sum(before, arrived, local):
    tiles, rows, points = local.shape
    return pl.pallas_call(
        last_body,
        out_shape=(
            jax.ShapeDtypeStruct((tiles, rows, points), jnp.bfloat16),
            jax.ShapeDtypeStruct((1, rows, points), jnp.bfloat16),
            jax.ShapeDtypeStruct((1, rows, points), jnp.bfloat16),
        ),
        in_specs=[SMEM, VMEM, VMEM],
        out_specs=(VMEM, VMEM, VMEM),
        scratch_shapes=[
            pltpu.VMEM((tiles + 1, rows, points), jnp.float32),
        ],
        compiler_params=SMALL,
    )(placed(before, pltpu.SMEM), placed(arrived, pltpu.VMEM), placed(local, pltpu.VMEM))


def stretch_tile(ndays, here, dy):
    rows, points = here.shape
    half = rows // 2
    lane = lax.broadcasted_iota(jnp.int32, (rows, points), 1)
    right = pltpu.roll(here, points - 1, 1)
    left = pltpu.roll(here, 1, 1)
    dx = jnp.where(lane == 0, right - here, jnp.where(lane == points - 1, here - left, (right - left) * 0.5))
    a, c = dx[:half], dx[half:]
    b, e = dy[:half], dy[half:]
    c11 = a * a + c * c
    c12 = a * b + c * e
    c22 = b * b + e * e
    gap = c11 - c22
    major = 0.5 * (c11 + c22 + jnp.sqrt(gap * gap + 4.0 * c12 * c12))
    lead = jnp.maximum(major, 1.0)
    det = a * e - b * c
    return jnp.log(lead) / (2.0 * ndays), det * det / lead


def inner_body(ndays, final_ref, ftle_ref, minor_ref):
    tiles, rows, points = final_ref.shape
    for t in range(1, tiles - 1):
        here = final_ref[t].astype(jnp.float32)
        dy = (final_ref[t + 1].astype(jnp.float32) - final_ref[t - 1].astype(jnp.float32)) * 0.5
        at = slice(t * points, (t + 1) * points)
        ftle_ref[:, at], minor_ref[:, at] = stretch_tile(ndays, here, dy)


def edge_body(ndays, final_ref, low_ref, high_ref, ftle_in, minor_in, ftle_ref, minor_ref, ftle_scr, minor_scr, sems):
    tiles, rows, points = final_ref.shape
    copies = []
    for i, t in enumerate((0, tiles - 1)):
        here = final_ref[t].astype(jnp.float32)
        below = (final_ref[t - 1] if t > 0 else low_ref[0]).astype(jnp.float32)
        above = (final_ref[t + 1] if t < tiles - 1 else high_ref[0]).astype(jnp.float32)
        one_sided = above - here if t == 0 else here - below
        at_end = lax.axis_index("tile") == (0 if t == 0 else lax.axis_size("tile") - 1)
        dy = jnp.where(at_end, one_sided, (above - below) * 0.5)
        ftle_scr[i], minor_scr[i] = stretch_tile(ndays, here, dy)
        at = pl.ds(t * points, points)
        for n, (scr, ref) in enumerate(((ftle_scr, ftle_ref), (minor_scr, minor_ref))):
            copy = pltpu.make_async_copy(scr.at[i], ref.at[:, at], sems.at[2 * i + n])
            copy.start()
            copies.append(copy)
    for copy in copies:
        copy.wait()


def stretch_inner(final, ndays):
    tiles, rows, points = final.shape
    shape = jax.ShapeDtypeStruct((rows // 2, tiles * points), jnp.float32)
    return pl.pallas_call(
        functools.partial(inner_body, float(ndays)),
        out_shape=(shape, shape),
        in_specs=[VMEM],
        out_specs=(VMEM, VMEM),
        compiler_params=SMALL,
        cost_estimate=pl.CostEstimate(flops=40 * rows * tiles * points, bytes_accessed=2 << 20, transcendentals=0),
    )(final)


def stretch_edges(final, low, high, inner, ndays):
    tiles, rows, points = final.shape
    shape = jax.ShapeDtypeStruct((rows // 2, tiles * points), jnp.float32)
    scr = pltpu.VMEM((2, rows // 2, points), jnp.float32)
    return pl.pallas_call(
        functools.partial(edge_body, float(ndays)),
        out_shape=(shape, shape),
        in_specs=[VMEM, VMEM, VMEM, HBM, HBM],
        out_specs=(HBM, HBM),
        scratch_shapes=[scr, scr, pltpu.SemaphoreType.DMA((4,))],
        input_output_aliases={3: 0, 4: 1},
        compiler_params=SMALL,
    )(final, low, high, *inner)


def own_rows(dest, me, tiles, peers, nnz):
    off = dest[:, 1:].reshape(tiles * (nnz - 1))
    peer = jnp.arange(peers, dtype=jnp.int32)
    order = jnp.arange(tiles * (nnz - 1), dtype=jnp.int32)
    wanted = jnp.max(jnp.where(off[None, :] // tiles == peer[:, None], order, 0), axis=1)
    home = jnp.where(off // tiles == me, off % tiles, tiles)
    return wanted, home


def body(seeds, blocks, dest_tiles):
    tiles, nnz, points = blocks.shape[1:4]
    width = seeds.shape[2]
    ndays, peers = lax.axis_size("day"), lax.axis_size("tile")
    me = lax.axis_index("tile")
    seeds = seeds.reshape(tiles, points, width)
    wblk = blocks[0]
    onward = functools.partial(lax.ppermute, axis_name="day", perm=shifted(ndays, -1))

    for step in range(ndays):
        if step == 0:
            out, state = send_first(dest_tiles.transpose(2, 0, 1), seeds, wblk, peers)
            dest, state = lax.optimization_barrier((dest_tiles[0], state))
            rows = own_rows(dest, me, tiles, peers, nnz)
            table = jnp.stack([*rows, jnp.zeros_like(rows[0])])
        else:
            out, state = send(quick, arrived, local, off)
        arrived = lax.all_to_all(out, "tile", split_axis=0, concat_axis=0, tiled=True)
        local = keep(table, state, wblk)
        given = table = onward(table)
        if step == 0:
            own = lax.broadcasted_iota(jnp.int32, (peers,), 0) == me
            landed = jnp.where(own, tiles, arrived[:, width, 0].astype(jnp.int32))
            table = jnp.concatenate([table[:2], landed[None]], axis=0)
        if step < ndays - 1:
            wblk = onward(wblk)
            wblk, local = lax.optimization_barrier((wblk, local))
            off, quick = fetch(wblk, table if step else given)
    final, lowest, highest = last_sum(hold(table), arrived, local)
    low = lax.ppermute(highest, "tile", [(i, i + 1) for i in range(peers - 1)])
    high = lax.ppermute(lowest, "tile", [(i + 1, i) for i in range(peers - 1)])
    inner = stretch_inner(final, ndays)
    ftle, minor = stretch_edges(final, low, high, inner, ndays)
    return ftle[None], minor[None]


def solution(mesh):
    in_specs = (P("day", "tile", None), P("day", "tile", None, None, None), P("day", "tile", None))
    out_specs = (P("day", None, "tile"), P("day", None, "tile"))
    return jax.shard_map(body, mesh=mesh, in_specs=in_specs, out_specs=out_specs, check_vma=False)
```

```python
import functools

import jax
import jax.numpy as jnp
from jax import lax
from jax.experimental import pallas as pl
from jax.experimental.pallas import tpu as pltpu
from jax.sharding import PartitionSpec as P

VMEM = pl.BlockSpec(memory_space=pltpu.VMEM)
SMEM = pl.BlockSpec(memory_space=pltpu.SMEM)
HBM = pl.BlockSpec(memory_space=pltpu.HBM)
SEND = pltpu.CompilerParams(vmem_limit_bytes=24 * 1024 * 1024)
KEEP = pltpu.CompilerParams(vmem_limit_bytes=24 * 1024 * 1024)
SMALL = pltpu.CompilerParams(vmem_limit_bytes=16 * 1024 * 1024)
PART = 4
SAYS = 16
SLOT, HOME, LANDED = range(3)


def shifted(n, by):
    return [(i, (i + by) % n) for i in range(n)]


def product(v, block):
    return lax.dot_general(v, block, (((1,), (1,)), ((), ())), preferred_element_type=jnp.float32)


def send_products(wanted, off_ref, state_ref, out_ref, stage, out_sems):
    rows, each = state_ref.shape[1], off_ref.shape[1]
    copies = []
    for p in range(stage.shape[0]):
        number = wanted(p)
        stage[p, :rows] = product(state_ref[lax.div(number, each)], off_ref[lax.div(number, each), lax.rem(number, each)]).astype(jnp.bfloat16)
        if p % PART == PART - 1:
            part = pl.ds(p + 1 - PART, PART)
            copy = pltpu.make_async_copy(stage.at[part], out_ref.at[part], out_sems.at[p // PART])
            copy.start()
            copies.append(copy)
    for copy in copies:
        copy.wait()


def add_arrived(landed, arrived_ref, gathered):
    gathered[...] = jnp.zeros_like(gathered)
    rows = gathered.shape[1]
    for p in range(arrived_ref.shape[0]):
        home = landed(p)
        gathered[home] = gathered[home] + arrived_ref[p, :rows].astype(jnp.float32)


def off_copy(blocks_ref, off_scr, sem):
    return pltpu.make_async_copy(blocks_ref.at[:, pl.ds(1, off_scr.shape[1])], off_scr, sem)


def first_body(
    dest_ref, seeds_ref, blocks_ref, out_ref, state_ref, seeds_scr, off_scr, stage, state_scr, dest, lists, sems, out_sems, in_sems
):
    nnz, _, tiles = dest.shape
    read = pltpu.make_async_copy(dest_ref, dest, sems.at[2])
    read.start()
    each = nnz - 1
    rows = state_scr.shape[1]
    parts = [pl.ds(t, PART) for t in range(0, tiles, PART)]
    seeding = [pltpu.make_async_copy(seeds_ref.at[p], seeds_scr.at[p], in_sems.at[n]) for n, p in enumerate(parts)]
    load = off_copy(blocks_ref, off_scr, sems.at[0])
    for copy in [*seeding, load]:
        copy.start()
    for t in range(tiles):
        if t % PART == 0:
            seeding[t // PART].wait()
        state_scr[t] = jnp.transpose(seeds_scr[t])
    store = pltpu.make_async_copy(state_scr, state_ref, sems.at[1])
    store.start()
    read.wait()
    for p in range(stage.shape[0]):
        lists[0, p] = 0
        lists[1, p] = tiles
    for t in range(tiles):
        for k in range(1, nnz):
            to = dest[k, 0, t]
            peer = lax.div(to, tiles)
            lists[0, peer] = t * each + k - 1
            lists[1, peer] = to - peer * tiles
    for p in range(stage.shape[0]):
        stage[p, rows:] = jnp.full((SAYS, stage.shape[2]), lists[1, p], jnp.int32).astype(jnp.float32).astype(jnp.bfloat16)
    load.wait()
    send_products(lambda p: lists[0, p], off_scr, state_scr, out_ref, stage, out_sems)
    store.wait()


def send_first(dest, seeds, blocks, peers):
    tiles, nnz, points = blocks.shape[:3]
    rows = seeds.shape[2]
    return pl.pallas_call(
        first_body,
        out_shape=(
            pltpu.HBM((peers, rows + SAYS, points), jnp.bfloat16),
            pltpu.HBM((tiles, rows, points), jnp.bfloat16),
        ),
        in_specs=[HBM, HBM, HBM],
        out_specs=(HBM, HBM),
        scratch_shapes=[
            pltpu.VMEM(seeds.shape, jnp.bfloat16),
            pltpu.VMEM((tiles, nnz - 1, points, points), jnp.bfloat16),
            pltpu.VMEM((peers, rows + SAYS, points), jnp.bfloat16),
            pltpu.VMEM((tiles, rows, points), jnp.bfloat16),
            pltpu.SMEM(dest.shape, jnp.int32),
            pltpu.SMEM((2, peers), jnp.int32),
            pltpu.SemaphoreType.DMA((3,)),
            pltpu.SemaphoreType.DMA((peers // PART,)),
            pltpu.SemaphoreType.DMA((tiles // PART,)),
        ],
        compiler_params=SEND,
        cost_estimate=pl.CostEstimate(
            flops=2 * peers * points * points * rows, bytes_accessed=4 << 20, transcendentals=0
        ),
    )(placed(dest, pltpu.HBM), placed(seeds, pltpu.HBM), placed(blocks, pltpu.HBM))


def fetch_body(blocks_ref, table_ref, off_ref, read_ref, sems):
    loads = [off_copy(blocks_ref, off_ref, sems.at[0]), pltpu.make_async_copy(table_ref, read_ref, sems.at[1])]
    for load in loads:
        load.start()
    for load in loads:
        load.wait()


def fetch(blocks, table):
    tiles, nnz, points = blocks.shape[:3]
    return pl.pallas_call(
        fetch_body,
        out_shape=(
            pltpu.VMEM((tiles, nnz - 1, points, points), jnp.bfloat16),
            pltpu.SMEM(table.shape, jnp.int32),
        ),
        in_specs=[HBM, HBM],
        out_specs=(VMEM, SMEM),
        scratch_shapes=[pltpu.SemaphoreType.DMA((2,))],
        compiler_params=SMALL,
        cost_estimate=pl.CostEstimate(flops=0, bytes_accessed=2 << 20, transcendentals=0),
    )(placed(blocks, pltpu.HBM), placed(table, pltpu.HBM))


def hold_body(table_ref, read_ref, sem):
    load = pltpu.make_async_copy(table_ref, read_ref, sem)
    load.start()
    load.wait()


def hold(table):
    return pl.pallas_call(
        hold_body,
        out_shape=pltpu.SMEM(table.shape, jnp.int32),
        in_specs=[HBM],
        out_specs=SMEM,
        scratch_shapes=[pltpu.SemaphoreType.DMA],
        compiler_params=SMALL,
        cost_estimate=pl.CostEstimate(flops=0, bytes_accessed=1 << 10, transcendentals=0),
    )(placed(table, pltpu.HBM))


def send_body(
    table, arrived_ref, local_ref, off_ref, out_ref, state_ref, stage, gathered, state_scr, store_sem, out_sems, *told,
):
    landed = lambda p: table[LANDED, p]
    if told:
        said, read, sem = told
        said[...] = arrived_ref[:, state_scr.shape[1], :].astype(jnp.float32).astype(jnp.int32)
        copy = pltpu.make_async_copy(said, read, sem)
        copy.start()
        copy.wait()
        me = lax.axis_index("tile")
        landed = lambda p: jnp.where(me == p, state_scr.shape[0], read[p, 0])
    add_arrived(landed, arrived_ref, gathered)
    for t in range(state_scr.shape[0]):
        state_scr[t] = (gathered[t] + local_ref[t]).astype(jnp.bfloat16)
    store = pltpu.make_async_copy(state_scr, state_ref, store_sem)
    store.start()
    each, points = off_ref.shape[1:3]
    copies = []
    for t in range(state_scr.shape[0]):
        both = product(state_scr[t], off_ref[t].reshape(each * points, off_ref.shape[3])).astype(jnp.bfloat16)
        for k in range(each):
            n = t * each + k
            stage[n] = both[:, k * points : (k + 1) * points]
            copy = pltpu.make_async_copy(stage.at[n], out_ref.at[table[SLOT, n]], out_sems.at[n])
            copy.start()
            copies.append(copy)
    for copy in copies:
        copy.wait()
    store.wait()


placed = pltpu.with_memory_space_constraint


def send(table, arrived, local, off):
    peers = arrived.shape[0]
    tiles, rows, points = local.shape
    told = []
    if arrived.shape[1] > rows:
        told = [pltpu.VMEM((peers, points), jnp.int32), pltpu.SMEM((peers, points), jnp.int32), pltpu.SemaphoreType.DMA]
    return pl.pallas_call(
        send_body,
        out_shape=(
            pltpu.HBM((peers, rows, points), jnp.bfloat16),
            pltpu.HBM((tiles, rows, points), jnp.bfloat16),
        ),
        in_specs=[SMEM, VMEM, VMEM, VMEM],
        out_specs=(HBM, HBM),
        scratch_shapes=[
            pltpu.VMEM((peers, rows, points), jnp.bfloat16),
            pltpu.VMEM((tiles + 1, rows, points), jnp.float32),
            pltpu.VMEM((tiles, rows, points), jnp.bfloat16),
            pltpu.SemaphoreType.DMA,
            pltpu.SemaphoreType.DMA((peers,)),
            *told,
        ],
        compiler_params=SEND,
        cost_estimate=pl.CostEstimate(
            flops=2 * peers * points * points * rows, bytes_accessed=4 << 20, transcendentals=0
        ),
    )(placed(table, pltpu.SMEM), placed(arrived, pltpu.VMEM), placed(local, pltpu.VMEM), placed(off, pltpu.VMEM))


def keep_body(table, state_ref, blocks_ref, local_ref, total, blocks_scr, sem):
    load = pltpu.make_async_copy(blocks_ref, blocks_scr, sem)
    load.start()
    load.wait()
    tiles, nnz = blocks_scr.shape[:2]
    for t in range(tiles):
        total[t] = product(state_ref[t], blocks_scr[t, 0])
    for t in range(tiles):
        for k in range(1, nnz):
            home = table[HOME, t * (nnz - 1) + k - 1]
            total[home] = total[home] + product(state_ref[t], blocks_scr[t, k])
    local_ref[...] = total[pl.ds(0, tiles)]


def keep(table, state, blocks):
    tiles, rows, points = state.shape
    return pl.pallas_call(
        keep_body,
        out_shape=pltpu.VMEM((tiles, rows, points), jnp.float32),
        in_specs=[SMEM, VMEM, HBM],
        out_specs=VMEM,
        scratch_shapes=[
            pltpu.VMEM((tiles + 1, rows, points), jnp.float32),
            pltpu.VMEM(blocks.shape, jnp.bfloat16),
            pltpu.SemaphoreType.DMA,
        ],
        compiler_params=KEEP,
        cost_estimate=pl.CostEstimate(
            flops=2 * tiles * blocks.shape[1] * points * points * rows, bytes_accessed=4 << 20, transcendentals=0
        ),
    )(table, placed(state, pltpu.HBM), placed(blocks, pltpu.HBM))


def last_body(before, arrived_ref, local_ref, final_ref, low_ref, high_ref, gathered):
    add_arrived(lambda p: before[LANDED, p], arrived_ref, gathered)
    tiles = final_ref.shape[0]
    for t in range(tiles):
        final_ref[t] = (gathered[t] + local_ref[t]).astype(jnp.bfloat16)
    low_ref[0] = final_ref[0]
    high_ref[0] = final_ref[tiles - 1]


def last_sum(before, arrived, local):
    tiles, rows, points = local.shape
    return pl.pallas_call(
        last_body,
        out_shape=(
            jax.ShapeDtypeStruct((tiles, rows, points), jnp.bfloat16),
            jax.ShapeDtypeStruct((1, rows, points), jnp.bfloat16),
            jax.ShapeDtypeStruct((1, rows, points), jnp.bfloat16),
        ),
        in_specs=[SMEM, VMEM, VMEM],
        out_specs=(VMEM, VMEM, VMEM),
        scratch_shapes=[
            pltpu.VMEM((tiles + 1, rows, points), jnp.float32),
        ],
        compiler_params=SMALL,
    )(placed(before, pltpu.SMEM), placed(arrived, pltpu.VMEM), placed(local, pltpu.VMEM))


def stretch_tile(ndays, here, dy):
    rows, points = here.shape
    half = rows // 2
    lane = lax.broadcasted_iota(jnp.int32, (rows, points), 1)
    right = pltpu.roll(here, points - 1, 1)
    left = pltpu.roll(here, 1, 1)
    dx = jnp.where(lane == 0, right - here, jnp.where(lane == points - 1, here - left, (right - left) * 0.5))
    a, c = dx[:half], dx[half:]
    b, e = dy[:half], dy[half:]
    c11 = a * a + c * c
    c12 = a * b + c * e
    c22 = b * b + e * e
    gap = c11 - c22
    major = 0.5 * (c11 + c22 + jnp.sqrt(gap * gap + 4.0 * c12 * c12))
    lead = jnp.maximum(major, 1.0)
    det = a * e - b * c
    return jnp.log(lead) / (2.0 * ndays), det * det / lead


def inner_body(ndays, final_ref, ftle_ref, minor_ref):
    tiles, rows, points = final_ref.shape
    for t in range(1, tiles - 1):
        here = final_ref[t].astype(jnp.float32)
        dy = (final_ref[t + 1].astype(jnp.float32) - final_ref[t - 1].astype(jnp.float32)) * 0.5
        at = slice(t * points, (t + 1) * points)
        ftle_ref[:, at], minor_ref[:, at] = stretch_tile(ndays, here, dy)


def edge_body(ndays, final_ref, low_ref, high_ref, ftle_in, minor_in, ftle_ref, minor_ref, ftle_scr, minor_scr, sems):
    tiles, rows, points = final_ref.shape
    copies = []
    for i, t in enumerate((0, tiles - 1)):
        here = final_ref[t].astype(jnp.float32)
        below = (final_ref[t - 1] if t > 0 else low_ref[0]).astype(jnp.float32)
        above = (final_ref[t + 1] if t < tiles - 1 else high_ref[0]).astype(jnp.float32)
        one_sided = above - here if t == 0 else here - below
        at_end = lax.axis_index("tile") == (0 if t == 0 else lax.axis_size("tile") - 1)
        dy = jnp.where(at_end, one_sided, (above - below) * 0.5)
        ftle_scr[i], minor_scr[i] = stretch_tile(ndays, here, dy)
        at = pl.ds(t * points, points)
        for n, (scr, ref) in enumerate(((ftle_scr, ftle_ref), (minor_scr, minor_ref))):
            copy = pltpu.make_async_copy(scr.at[i], ref.at[:, at], sems.at[2 * i + n])
            copy.start()
            copies.append(copy)
    for copy in copies:
        copy.wait()


def stretch_inner(final, ndays):
    tiles, rows, points = final.shape
    shape = jax.ShapeDtypeStruct((rows // 2, tiles * points), jnp.float32)
    return pl.pallas_call(
        functools.partial(inner_body, float(ndays)),
        out_shape=(shape, shape),
        in_specs=[VMEM],
        out_specs=(VMEM, VMEM),
        compiler_params=SMALL,
        cost_estimate=pl.CostEstimate(flops=40 * rows * tiles * points, bytes_accessed=2 << 20, transcendentals=0),
    )(final)


def stretch_edges(final, low, high, inner, ndays):
    tiles, rows, points = final.shape
    shape = jax.ShapeDtypeStruct((rows // 2, tiles * points), jnp.float32)
    scr = pltpu.VMEM((2, rows // 2, points), jnp.float32)
    return pl.pallas_call(
        functools.partial(edge_body, float(ndays)),
        out_shape=(shape, shape),
        in_specs=[VMEM, VMEM, VMEM, HBM, HBM],
        out_specs=(HBM, HBM),
        scratch_shapes=[scr, scr, pltpu.SemaphoreType.DMA((4,))],
        input_output_aliases={3: 0, 4: 1},
        compiler_params=SMALL,
    )(final, low, high, *inner)


def own_rows(dest, me, tiles, peers, nnz):
    off = dest[:, 1:].reshape(tiles * (nnz - 1))
    dev = off // tiles
    stays = dev == me
    home = jnp.where(stays, off % tiles, tiles)
    peer = jnp.arange(peers, dtype=jnp.int32)
    order = jnp.arange(off.shape[0], dtype=jnp.int32)
    free = jnp.logical_not(jnp.any((dev[None, :] == peer[:, None]) & jnp.logical_not(stays)[None, :], axis=1))
    stayed = jnp.sum(jnp.where(order[None, :] < order[:, None], stays[None, :], False).astype(jnp.int32), axis=1)
    frees = jnp.sum(jnp.where(peer[None, :] < peer[:, None], free[None, :], False).astype(jnp.int32), axis=1)
    taken = (stayed[:, None] == frees[None, :]) & free[None, :]
    slot = jnp.where(stays, jnp.sum(jnp.where(taken, peer[None, :], 0), axis=1), dev)
    return slot, home


def body(seeds, blocks, dest_tiles):
    tiles, nnz, points = blocks.shape[1:4]
    width = seeds.shape[2]
    ndays, peers = lax.axis_size("day"), lax.axis_size("tile")
    me = lax.axis_index("tile")
    seeds = seeds.reshape(tiles, points, width)
    wblk = blocks[0]
    onward = functools.partial(lax.ppermute, axis_name="day", perm=shifted(ndays, -1))

    for step in range(ndays):
        if step == 0:
            out, state = send_first(dest_tiles.transpose(2, 0, 1), seeds, wblk, peers)
            dest, state = lax.optimization_barrier((dest_tiles[0], state))
            rows = own_rows(dest, me, tiles, peers, nnz)
            table = jnp.stack([*rows, jnp.zeros_like(rows[0])])
        else:
            out, state = send(quick, arrived, local, off)
        arrived = lax.all_to_all(out, "tile", split_axis=0, concat_axis=0, tiled=True)
        local = keep(table, state, wblk)
        given = table = onward(table)
        if step == 0:
            own = lax.broadcasted_iota(jnp.int32, (peers,), 0) == me
            landed = jnp.where(own, tiles, arrived[:, width, 0].astype(jnp.int32))
            table = jnp.concatenate([table[:2], landed[None]], axis=0)
        if step < ndays - 1:
            wblk = onward(wblk)
            wblk, local = lax.optimization_barrier((wblk, local))
            off, quick = fetch(wblk, table if step else given)
    final, lowest, highest = last_sum(hold(table), arrived, local)
    low = lax.ppermute(highest, "tile", [(i, i + 1) for i in range(peers - 1)])
    high = lax.ppermute(lowest, "tile", [(i + 1, i) for i in range(peers - 1)])
    inner = stretch_inner(final, ndays)
    ftle, minor = stretch_edges(final, low, high, inner, ndays)
    return ftle[None], minor[None]


def solution(mesh):
    in_specs = (P("day", "tile", None), P("day", "tile", None, None, None), P("day", "tile", None))
    out_specs = (P("day", None, "tile"), P("day", None, "tile"))
    return jax.shard_map(body, mesh=mesh, in_specs=in_specs, out_specs=out_specs, check_vma=False)
```

```python
import functools

import jax
import jax.numpy as jnp
from jax import lax
from jax.experimental import pallas as pl
from jax.experimental.pallas import tpu as pltpu
from jax.sharding import PartitionSpec as P

VMEM = pl.BlockSpec(memory_space=pltpu.VMEM)
SMEM = pl.BlockSpec(memory_space=pltpu.SMEM)
HBM = pl.BlockSpec(memory_space=pltpu.HBM)
SEND = pltpu.CompilerParams(vmem_limit_bytes=24 * 1024 * 1024)
KEEP = pltpu.CompilerParams(vmem_limit_bytes=24 * 1024 * 1024)
SMALL = pltpu.CompilerParams(vmem_limit_bytes=16 * 1024 * 1024)
PART = 4
SAYS = 16
SLOT, HOME, LANDED = range(3)


def shifted(n, by):
    return [(i, (i + by) % n) for i in range(n)]


def product(v, block):
    return lax.dot_general(v, block, (((1,), (1,)), ((), ())), preferred_element_type=jnp.float32)


def send_products(wanted, off_ref, state_ref, out_ref, stage, out_sems):
    rows, each = state_ref.shape[1], off_ref.shape[1]
    copies = []
    for p in range(stage.shape[0]):
        number = wanted(p)
        stage[p, :rows] = product(state_ref[lax.div(number, each)], off_ref[lax.div(number, each), lax.rem(number, each)]).astype(jnp.bfloat16)
        if p % PART == PART - 1:
            part = pl.ds(p + 1 - PART, PART)
            copy = pltpu.make_async_copy(stage.at[part], out_ref.at[part], out_sems.at[p // PART])
            copy.start()
            copies.append(copy)
    for copy in copies:
        copy.wait()


def add_arrived(landed, arrived_ref, gathered):
    gathered[...] = jnp.zeros_like(gathered)
    rows = gathered.shape[1]
    for p in range(arrived_ref.shape[0]):
        home = landed(p)
        gathered[home] = gathered[home] + arrived_ref[p, :rows].astype(jnp.float32)


def off_copy(blocks_ref, off_scr, sem):
    return pltpu.make_async_copy(blocks_ref.at[:, pl.ds(1, off_scr.shape[1])], off_scr, sem)


def first_body(
    dest_ref, seeds_ref, blocks_ref, out_ref, state_ref, seeds_scr, off_scr, stage, state_scr, dest, lists, sems, out_sems, in_sems
):
    nnz, _, tiles = dest.shape
    read = pltpu.make_async_copy(dest_ref, dest, sems.at[2])
    read.start()
    each = nnz - 1
    rows = state_scr.shape[1]
    parts = [pl.ds(t, PART) for t in range(0, tiles, PART)]
    seeding = [pltpu.make_async_copy(seeds_ref.at[p], seeds_scr.at[p], in_sems.at[n]) for n, p in enumerate(parts)]
    load = off_copy(blocks_ref, off_scr, sems.at[0])
    for copy in [*seeding, load]:
        copy.start()
    for t in range(tiles):
        if t % PART == 0:
            seeding[t // PART].wait()
        state_scr[t] = jnp.transpose(seeds_scr[t])
    store = pltpu.make_async_copy(state_scr, state_ref, sems.at[1])
    store.start()
    read.wait()
    for p in range(stage.shape[0]):
        lists[0, p] = 0
        lists[1, p] = tiles
    for t in range(tiles):
        for k in range(1, nnz):
            to = dest[k, 0, t]
            peer = lax.div(to, tiles)
            lists[0, peer] = t * each + k - 1
            lists[1, peer] = to - peer * tiles
    for p in range(stage.shape[0]):
        stage[p, rows:] = jnp.full((SAYS, stage.shape[2]), lists[1, p], jnp.int32).astype(jnp.float32).astype(jnp.bfloat16)
    load.wait()
    send_products(lambda p: lists[0, p], off_scr, state_scr, out_ref, stage, out_sems)
    store.wait()


def send_first(dest, seeds, blocks, peers):
    tiles, nnz, points = blocks.shape[:3]
    rows = seeds.shape[2]
    return pl.pallas_call(
        first_body,
        out_shape=(
            pltpu.HBM((peers, rows + SAYS, points), jnp.bfloat16),
            pltpu.HBM((tiles, rows, points), jnp.bfloat16),
        ),
        in_specs=[HBM, HBM, HBM],
        out_specs=(HBM, HBM),
        scratch_shapes=[
            pltpu.VMEM(seeds.shape, jnp.bfloat16),
            pltpu.VMEM((tiles, nnz - 1, points, points), jnp.bfloat16),
            pltpu.VMEM((peers, rows + SAYS, points), jnp.bfloat16),
            pltpu.VMEM((tiles, rows, points), jnp.bfloat16),
            pltpu.SMEM(dest.shape, jnp.int32),
            pltpu.SMEM((2, peers), jnp.int32),
            pltpu.SemaphoreType.DMA((3,)),
            pltpu.SemaphoreType.DMA((peers // PART,)),
            pltpu.SemaphoreType.DMA((tiles // PART,)),
        ],
        compiler_params=SEND,
        cost_estimate=pl.CostEstimate(
            flops=2 * peers * points * points * rows, bytes_accessed=4 << 20, transcendentals=0
        ),
    )(placed(dest, pltpu.HBM), placed(seeds, pltpu.HBM), placed(blocks, pltpu.HBM))


def fetch_body(blocks_ref, table_ref, off_ref, read_ref, sems):
    loads = [off_copy(blocks_ref, off_ref, sems.at[0]), pltpu.make_async_copy(table_ref, read_ref, sems.at[1])]
    for load in loads:
        load.start()
    for load in loads:
        load.wait()


def fetch(blocks, table):
    tiles, nnz, points = blocks.shape[:3]
    return pl.pallas_call(
        fetch_body,
        out_shape=(
            pltpu.VMEM((tiles, nnz - 1, points, points), jnp.bfloat16),
            pltpu.SMEM(table.shape, jnp.int32),
        ),
        in_specs=[HBM, HBM],
        out_specs=(VMEM, SMEM),
        scratch_shapes=[pltpu.SemaphoreType.DMA((2,))],
        compiler_params=SMALL,
        cost_estimate=pl.CostEstimate(flops=0, bytes_accessed=2 << 20, transcendentals=0),
    )(placed(blocks, pltpu.HBM), placed(table, pltpu.HBM))


def hold_body(table_ref, read_ref, sem):
    load = pltpu.make_async_copy(table_ref, read_ref, sem)
    load.start()
    load.wait()


def hold(table):
    return pl.pallas_call(
        hold_body,
        out_shape=pltpu.SMEM(table.shape, jnp.int32),
        in_specs=[HBM],
        out_specs=SMEM,
        scratch_shapes=[pltpu.SemaphoreType.DMA],
        compiler_params=SMALL,
        cost_estimate=pl.CostEstimate(flops=0, bytes_accessed=1 << 10, transcendentals=0),
    )(placed(table, pltpu.HBM))


def send_body(
    table, arrived_ref, local_ref, off_ref, out_ref, state_ref, stage, gathered, state_scr, store_sem, out_sems, *told,
):
    landed = lambda p: table[LANDED, p]
    if told:
        said, read, sem = told
        says = arrived_ref[:, state_scr.shape[1] :].astype(jnp.float32)
        said[...] = jnp.max(says, axis=1).astype(jnp.int32)
        copy = pltpu.make_async_copy(said, read, sem)
        copy.start()
        copy.wait()
        me = lax.axis_index("tile")
        landed = lambda p: jnp.where(me == p, state_scr.shape[0], read[p, 0])
    add_arrived(landed, arrived_ref, gathered)
    for t in range(state_scr.shape[0]):
        state_scr[t] = (gathered[t] + local_ref[t]).astype(jnp.bfloat16)
    store = pltpu.make_async_copy(state_scr, state_ref, store_sem)
    store.start()
    each, points = off_ref.shape[1:3]
    copies = []
    for t in range(state_scr.shape[0]):
        both = product(state_scr[t], off_ref[t].reshape(each * points, off_ref.shape[3])).astype(jnp.bfloat16)
        for k in range(each):
            n = t * each + k
            stage[n] = both[:, k * points : (k + 1) * points]
            copy = pltpu.make_async_copy(stage.at[n], out_ref.at[table[SLOT, n]], out_sems.at[n])
            copy.start()
            copies.append(copy)
    for copy in copies:
        copy.wait()
    store.wait()


placed = pltpu.with_memory_space_constraint


def send(table, arrived, local, off):
    peers = arrived.shape[0]
    tiles, rows, points = local.shape
    told = []
    if arrived.shape[1] > rows:
        told = [pltpu.VMEM((peers, points), jnp.int32), pltpu.SMEM((peers, points), jnp.int32), pltpu.SemaphoreType.DMA]
    return pl.pallas_call(
        send_body,
        out_shape=(
            pltpu.HBM((peers, rows, points), jnp.bfloat16),
            pltpu.HBM((tiles, rows, points), jnp.bfloat16),
        ),
        in_specs=[SMEM, VMEM, VMEM, VMEM],
        out_specs=(HBM, HBM),
        scratch_shapes=[
            pltpu.VMEM((peers, rows, points), jnp.bfloat16),
            pltpu.VMEM((tiles + 1, rows, points), jnp.float32),
            pltpu.VMEM((tiles, rows, points), jnp.bfloat16),
            pltpu.SemaphoreType.DMA,
            pltpu.SemaphoreType.DMA((peers,)),
            *told,
        ],
        compiler_params=SEND,
        cost_estimate=pl.CostEstimate(
            flops=2 * peers * points * points * rows, bytes_accessed=4 << 20, transcendentals=0
        ),
    )(placed(table, pltpu.SMEM), placed(arrived, pltpu.VMEM), placed(local, pltpu.VMEM), placed(off, pltpu.VMEM))


def keep_body(table, state_ref, blocks_ref, local_ref, total, blocks_scr, sem):
    load = pltpu.make_async_copy(blocks_ref, blocks_scr, sem)
    load.start()
    load.wait()
    tiles, nnz = blocks_scr.shape[:2]
    for t in range(tiles):
        total[t] = product(state_ref[t], blocks_scr[t, 0])
    for t in range(tiles):
        for k in range(1, nnz):
            home = table[HOME, t * (nnz - 1) + k - 1]
            total[home] = total[home] + product(state_ref[t], blocks_scr[t, k])
    local_ref[...] = total[pl.ds(0, tiles)]


def keep(table, state, blocks):
    tiles, rows, points = state.shape
    return pl.pallas_call(
        keep_body,
        out_shape=pltpu.VMEM((tiles, rows, points), jnp.float32),
        in_specs=[SMEM, VMEM, HBM],
        out_specs=VMEM,
        scratch_shapes=[
            pltpu.VMEM((tiles + 1, rows, points), jnp.float32),
            pltpu.VMEM(blocks.shape, jnp.bfloat16),
            pltpu.SemaphoreType.DMA,
        ],
        compiler_params=KEEP,
        cost_estimate=pl.CostEstimate(
            flops=2 * tiles * blocks.shape[1] * points * points * rows, bytes_accessed=4 << 20, transcendentals=0
        ),
    )(table, placed(state, pltpu.HBM), placed(blocks, pltpu.HBM))


def last_body(before, arrived_ref, local_ref, final_ref, low_ref, high_ref, gathered):
    add_arrived(lambda p: before[LANDED, p], arrived_ref, gathered)
    tiles = final_ref.shape[0]
    for t in range(tiles):
        final_ref[t] = (gathered[t] + local_ref[t]).astype(jnp.bfloat16)
    low_ref[0] = final_ref[0]
    high_ref[0] = final_ref[tiles - 1]


def last_sum(before, arrived, local):
    tiles, rows, points = local.shape
    return pl.pallas_call(
        last_body,
        out_shape=(
            jax.ShapeDtypeStruct((tiles, rows, points), jnp.bfloat16),
            jax.ShapeDtypeStruct((1, rows, points), jnp.bfloat16),
            jax.ShapeDtypeStruct((1, rows, points), jnp.bfloat16),
        ),
        in_specs=[SMEM, VMEM, VMEM],
        out_specs=(VMEM, VMEM, VMEM),
        scratch_shapes=[
            pltpu.VMEM((tiles + 1, rows, points), jnp.float32),
        ],
        compiler_params=SMALL,
    )(placed(before, pltpu.SMEM), placed(arrived, pltpu.VMEM), placed(local, pltpu.VMEM))


def stretch_tile(ndays, here, dy):
    rows, points = here.shape
    half = rows // 2
    lane = lax.broadcasted_iota(jnp.int32, (rows, points), 1)
    right = pltpu.roll(here, points - 1, 1)
    left = pltpu.roll(here, 1, 1)
    dx = jnp.where(lane == 0, right - here, jnp.where(lane == points - 1, here - left, (right - left) * 0.5))
    a, c = dx[:half], dx[half:]
    b, e = dy[:half], dy[half:]
    c11 = a * a + c * c
    c12 = a * b + c * e
    c22 = b * b + e * e
    gap = c11 - c22
    major = 0.5 * (c11 + c22 + jnp.sqrt(gap * gap + 4.0 * c12 * c12))
    lead = jnp.maximum(major, 1.0)
    det = a * e - b * c
    return jnp.log(lead) / (2.0 * ndays), det * det / lead


def inner_body(ndays, final_ref, ftle_ref, minor_ref):
    tiles, rows, points = final_ref.shape
    for t in range(1, tiles - 1):
        here = final_ref[t].astype(jnp.float32)
        dy = (final_ref[t + 1].astype(jnp.float32) - final_ref[t - 1].astype(jnp.float32)) * 0.5
        at = slice(t * points, (t + 1) * points)
        ftle_ref[:, at], minor_ref[:, at] = stretch_tile(ndays, here, dy)


def edge_body(ndays, final_ref, low_ref, high_ref, ftle_in, minor_in, ftle_ref, minor_ref, ftle_scr, minor_scr, sems):
    tiles, rows, points = final_ref.shape
    copies = []
    for i, t in enumerate((0, tiles - 1)):
        here = final_ref[t].astype(jnp.float32)
        below = (final_ref[t - 1] if t > 0 else low_ref[0]).astype(jnp.float32)
        above = (final_ref[t + 1] if t < tiles - 1 else high_ref[0]).astype(jnp.float32)
        one_sided = above - here if t == 0 else here - below
        at_end = lax.axis_index("tile") == (0 if t == 0 else lax.axis_size("tile") - 1)
        dy = jnp.where(at_end, one_sided, (above - below) * 0.5)
        ftle_scr[i], minor_scr[i] = stretch_tile(ndays, here, dy)
        at = pl.ds(t * points, points)
        for n, (scr, ref) in enumerate(((ftle_scr, ftle_ref), (minor_scr, minor_ref))):
            copy = pltpu.make_async_copy(scr.at[i], ref.at[:, at], sems.at[2 * i + n])
            copy.start()
            copies.append(copy)
    for copy in copies:
        copy.wait()


def stretch_inner(final, ndays):
    tiles, rows, points = final.shape
    shape = jax.ShapeDtypeStruct((rows // 2, tiles * points), jnp.float32)
    return pl.pallas_call(
        functools.partial(inner_body, float(ndays)),
        out_shape=(shape, shape),
        in_specs=[VMEM],
        out_specs=(VMEM, VMEM),
        compiler_params=SMALL,
        cost_estimate=pl.CostEstimate(flops=40 * rows * tiles * points, bytes_accessed=2 << 20, transcendentals=0),
    )(final)


def stretch_edges(final, low, high, inner, ndays):
    tiles, rows, points = final.shape
    shape = jax.ShapeDtypeStruct((rows // 2, tiles * points), jnp.float32)
    scr = pltpu.VMEM((2, rows // 2, points), jnp.float32)
    return pl.pallas_call(
        functools.partial(edge_body, float(ndays)),
        out_shape=(shape, shape),
        in_specs=[VMEM, VMEM, VMEM, HBM, HBM],
        out_specs=(HBM, HBM),
        scratch_shapes=[scr, scr, pltpu.SemaphoreType.DMA((4,))],
        input_output_aliases={3: 0, 4: 1},
        compiler_params=SMALL,
    )(final, low, high, *inner)


def own_rows(dest, me, tiles, peers, nnz):
    off = dest[:, 1:].reshape(tiles * (nnz - 1))
    dev = off // tiles
    stays = dev == me
    home = jnp.where(stays, off % tiles, tiles)
    peer = jnp.arange(peers, dtype=jnp.int32)
    order = jnp.arange(off.shape[0], dtype=jnp.int32)
    free = jnp.logical_not(jnp.any((dev[None, :] == peer[:, None]) & jnp.logical_not(stays)[None, :], axis=1))
    stayed = jnp.sum(jnp.where(order[None, :] < order[:, None], stays[None, :], False).astype(jnp.int32), axis=1)
    frees = jnp.sum(jnp.where(peer[None, :] < peer[:, None], free[None, :], False).astype(jnp.int32), axis=1)
    taken = (stayed[:, None] == frees[None, :]) & free[None, :]
    slot = jnp.where(stays, jnp.sum(jnp.where(taken, peer[None, :], 0), axis=1), dev)
    return slot, home


def body(seeds, blocks, dest_tiles):
    tiles, nnz, points = blocks.shape[1:4]
    width = seeds.shape[2]
    ndays, peers = lax.axis_size("day"), lax.axis_size("tile")
    me = lax.axis_index("tile")
    seeds = seeds.reshape(tiles, points, width)
    wblk = blocks[0]
    onward = functools.partial(lax.ppermute, axis_name="day", perm=shifted(ndays, -1))

    for step in range(ndays):
        if step == 0:
            out, state = send_first(dest_tiles.transpose(2, 0, 1), seeds, wblk, peers)
            dest, state = lax.optimization_barrier((dest_tiles[0], state))
            rows = own_rows(dest, me, tiles, peers, nnz)
            table = jnp.stack([*rows, jnp.zeros_like(rows[0])])
        else:
            out, state = send(quick, arrived, local, off)
        arrived = lax.all_to_all(out, "tile", split_axis=0, concat_axis=0, tiled=True)
        local = keep(table, state, wblk)
        given = table = onward(table)
        if step == 0:
            own = lax.broadcasted_iota(jnp.int32, (peers,), 0) == me
            landed = jnp.where(own, tiles, arrived[:, width, 0].astype(jnp.int32))
            table = jnp.concatenate([table[:2], landed[None]], axis=0)
        if step < ndays - 1:
            wblk = onward(wblk)
            wblk, local = lax.optimization_barrier((wblk, local))
            off, quick = fetch(wblk, table if step else given)
    final, lowest, highest = last_sum(hold(table), arrived, local)
    low = lax.ppermute(highest, "tile", [(i, i + 1) for i in range(peers - 1)])
    high = lax.ppermute(lowest, "tile", [(i + 1, i) for i in range(peers - 1)])
    inner = stretch_inner(final, ndays)
    ftle, minor = stretch_edges(final, low, high, inner, ndays)
    return ftle[None], minor[None]


def solution(mesh):
    in_specs = (P("day", "tile", None), P("day", "tile", None, None, None), P("day", "tile", None))
    out_specs = (P("day", None, "tile"), P("day", None, "tile"))
    return jax.shard_map(body, mesh=mesh, in_specs=in_specs, out_specs=out_specs, check_vma=False)
```

```python
import functools

import jax
import jax.numpy as jnp
from jax import lax
from jax.experimental import pallas as pl
from jax.experimental.pallas import tpu as pltpu
from jax.sharding import PartitionSpec as P

VMEM = pl.BlockSpec(memory_space=pltpu.VMEM)
SMEM = pl.BlockSpec(memory_space=pltpu.SMEM)
HBM = pl.BlockSpec(memory_space=pltpu.HBM)
SEND = pltpu.CompilerParams(vmem_limit_bytes=24 * 1024 * 1024)
KEEP = pltpu.CompilerParams(vmem_limit_bytes=24 * 1024 * 1024)
SMALL = pltpu.CompilerParams(vmem_limit_bytes=16 * 1024 * 1024)
PART = 4
SAYS = 16
SLOT, HOME, LANDED = range(3)


def shifted(n, by):
    return [(i, (i + by) % n) for i in range(n)]


def product(v, block):
    return lax.dot_general(v, block, (((1,), (1,)), ((), ())), preferred_element_type=jnp.float32)


def send_products(wanted, off_ref, state_ref, out_ref, stage, out_sems):
    rows, each = state_ref.shape[1], off_ref.shape[1]
    copies = []
    for p in range(stage.shape[0]):
        number = wanted(p)
        stage[p, :rows] = product(state_ref[lax.div(number, each)], off_ref[lax.div(number, each), lax.rem(number, each)]).astype(jnp.bfloat16)
        if p % PART == PART - 1:
            part = pl.ds(p + 1 - PART, PART)
            copy = pltpu.make_async_copy(stage.at[part], out_ref.at[part], out_sems.at[p // PART])
            copy.start()
            copies.append(copy)
    for copy in copies:
        copy.wait()


def add_arrived(landed, arrived_ref, local_ref, gathered):
    gathered[: local_ref.shape[0]] = local_ref[...]
    gathered[local_ref.shape[0]] = jnp.zeros(gathered.shape[1:], gathered.dtype)
    rows = gathered.shape[1]
    for p in range(arrived_ref.shape[0]):
        home = landed(p)
        gathered[home] = gathered[home] + arrived_ref[p, :rows].astype(jnp.float32)


def off_copy(blocks_ref, off_scr, sem):
    return pltpu.make_async_copy(blocks_ref.at[:, pl.ds(1, off_scr.shape[1])], off_scr, sem)


def first_body(
    dest_ref, seeds_ref, blocks_ref, out_ref, state_ref, seeds_scr, off_scr, stage, state_scr, dest, lists, sems, out_sems, in_sems
):
    nnz, _, tiles = dest.shape
    read = pltpu.make_async_copy(dest_ref, dest, sems.at[2])
    read.start()
    each = nnz - 1
    rows = state_scr.shape[1]
    parts = [pl.ds(t, PART) for t in range(0, tiles, PART)]
    seeding = [pltpu.make_async_copy(seeds_ref.at[p], seeds_scr.at[p], in_sems.at[n]) for n, p in enumerate(parts)]
    load = off_copy(blocks_ref, off_scr, sems.at[0])
    for copy in [*seeding, load]:
        copy.start()
    for t in range(tiles):
        if t % PART == 0:
            seeding[t // PART].wait()
        state_scr[t] = jnp.transpose(seeds_scr[t])
    store = pltpu.make_async_copy(state_scr, state_ref, sems.at[1])
    store.start()
    read.wait()
    for p in range(stage.shape[0]):
        lists[0, p] = 0
        lists[1, p] = tiles
    for t in range(tiles):
        for k in range(1, nnz):
            to = dest[k, 0, t]
            peer = lax.div(to, tiles)
            lists[0, peer] = t * each + k - 1
            lists[1, peer] = to - peer * tiles
    for p in range(stage.shape[0]):
        stage[p, rows:] = jnp.full((SAYS, stage.shape[2]), lists[1, p], jnp.int32).astype(jnp.float32).astype(jnp.bfloat16)
    load.wait()
    send_products(lambda p: lists[0, p], off_scr, state_scr, out_ref, stage, out_sems)
    store.wait()


def send_first(dest, seeds, blocks, peers):
    tiles, nnz, points = blocks.shape[:3]
    rows = seeds.shape[2]
    return pl.pallas_call(
        first_body,
        out_shape=(
            pltpu.HBM((peers, rows + SAYS, points), jnp.bfloat16),
            pltpu.HBM((tiles, rows, points), jnp.bfloat16),
        ),
        in_specs=[HBM, HBM, HBM],
        out_specs=(HBM, HBM),
        scratch_shapes=[
            pltpu.VMEM(seeds.shape, jnp.bfloat16),
            pltpu.VMEM((tiles, nnz - 1, points, points), jnp.bfloat16),
            pltpu.VMEM((peers, rows + SAYS, points), jnp.bfloat16),
            pltpu.VMEM((tiles, rows, points), jnp.bfloat16),
            pltpu.SMEM(dest.shape, jnp.int32),
            pltpu.SMEM((2, peers), jnp.int32),
            pltpu.SemaphoreType.DMA((3,)),
            pltpu.SemaphoreType.DMA((peers // PART,)),
            pltpu.SemaphoreType.DMA((tiles // PART,)),
        ],
        compiler_params=SEND,
        cost_estimate=pl.CostEstimate(
            flops=2 * peers * points * points * rows, bytes_accessed=4 << 20, transcendentals=0
        ),
    )(placed(dest, pltpu.HBM), placed(seeds, pltpu.HBM), placed(blocks, pltpu.HBM))


def fetch_body(blocks_ref, table_ref, off_ref, read_ref, sems):
    loads = [off_copy(blocks_ref, off_ref, sems.at[0]), pltpu.make_async_copy(table_ref, read_ref, sems.at[1])]
    for load in loads:
        load.start()
    for load in loads:
        load.wait()


def fetch(blocks, table):
    tiles, nnz, points = blocks.shape[:3]
    return pl.pallas_call(
        fetch_body,
        out_shape=(
            pltpu.VMEM((tiles, nnz - 1, points, points), jnp.bfloat16),
            pltpu.SMEM(table.shape, jnp.int32),
        ),
        in_specs=[HBM, HBM],
        out_specs=(VMEM, SMEM),
        scratch_shapes=[pltpu.SemaphoreType.DMA((2,))],
        compiler_params=SMALL,
        cost_estimate=pl.CostEstimate(flops=0, bytes_accessed=2 << 20, transcendentals=0),
    )(placed(blocks, pltpu.HBM), placed(table, pltpu.HBM))


def hold_body(table_ref, read_ref, sem):
    load = pltpu.make_async_copy(table_ref, read_ref, sem)
    load.start()
    load.wait()


def hold(table):
    return pl.pallas_call(
        hold_body,
        out_shape=pltpu.SMEM(table.shape, jnp.int32),
        in_specs=[HBM],
        out_specs=SMEM,
        scratch_shapes=[pltpu.SemaphoreType.DMA],
        compiler_params=SMALL,
        cost_estimate=pl.CostEstimate(flops=0, bytes_accessed=1 << 10, transcendentals=0),
    )(placed(table, pltpu.HBM))


def send_body(
    table, arrived_ref, local_ref, off_ref, out_ref, state_ref, stage, gathered, state_scr, store_sem, out_sems, *told,
):
    landed = lambda p: table[LANDED, p]
    if told:
        said, read, sem = told
        says = arrived_ref[:, state_scr.shape[1] :].astype(jnp.float32)
        said[...] = jnp.max(says, axis=1).astype(jnp.int32)
        copy = pltpu.make_async_copy(said, read, sem)
        copy.start()
        copy.wait()
        me = lax.axis_index("tile")
        landed = lambda p: jnp.where(me == p, state_scr.shape[0], read[p, 0])
    add_arrived(landed, arrived_ref, local_ref, gathered)
    for t in range(state_scr.shape[0]):
        state_scr[t] = gathered[t].astype(jnp.bfloat16)
    store = pltpu.make_async_copy(state_scr, state_ref, store_sem)
    store.start()
    each, points = off_ref.shape[1:3]
    copies = []
    for t in range(state_scr.shape[0]):
        both = product(state_scr[t], off_ref[t].reshape(each * points, off_ref.shape[3])).astype(jnp.bfloat16)
        for k in range(each):
            n = t * each + k
            stage[n] = both[:, k * points : (k + 1) * points]
            copy = pltpu.make_async_copy(stage.at[n], out_ref.at[table[SLOT, n]], out_sems.at[n])
            copy.start()
            copies.append(copy)
    for copy in copies:
        copy.wait()
    store.wait()


placed = pltpu.with_memory_space_constraint


def send(table, arrived, local, off):
    peers = arrived.shape[0]
    tiles, rows, points = local.shape
    told = []
    if arrived.shape[1] > rows:
        told = [pltpu.VMEM((peers, points), jnp.int32), pltpu.SMEM((peers, points), jnp.int32), pltpu.SemaphoreType.DMA]
    return pl.pallas_call(
        send_body,
        out_shape=(
            pltpu.HBM((peers, rows, points), jnp.bfloat16),
            pltpu.HBM((tiles, rows, points), jnp.bfloat16),
        ),
        in_specs=[SMEM, VMEM, VMEM, VMEM],
        out_specs=(HBM, HBM),
        scratch_shapes=[
            pltpu.VMEM((peers, rows, points), jnp.bfloat16),
            pltpu.VMEM((tiles + 1, rows, points), jnp.float32),
            pltpu.VMEM((tiles, rows, points), jnp.bfloat16),
            pltpu.SemaphoreType.DMA,
            pltpu.SemaphoreType.DMA((peers,)),
            *told,
        ],
        compiler_params=SEND,
        cost_estimate=pl.CostEstimate(
            flops=2 * peers * points * points * rows, bytes_accessed=4 << 20, transcendentals=0
        ),
    )(placed(table, pltpu.SMEM), placed(arrived, pltpu.VMEM), placed(local, pltpu.VMEM), placed(off, pltpu.VMEM))


def keep_body(table, state_ref, blocks_ref, local_ref, total, blocks_scr, sem):
    load = pltpu.make_async_copy(blocks_ref, blocks_scr, sem)
    load.start()
    load.wait()
    tiles, nnz = blocks_scr.shape[:2]
    for t in range(tiles):
        total[t] = product(state_ref[t], blocks_scr[t, 0])
    for t in range(tiles):
        for k in range(1, nnz):
            home = table[HOME, t * (nnz - 1) + k - 1]
            total[home] = total[home] + product(state_ref[t], blocks_scr[t, k])
    local_ref[...] = total[pl.ds(0, tiles)]


def keep(table, state, blocks):
    tiles, rows, points = state.shape
    return pl.pallas_call(
        keep_body,
        out_shape=pltpu.VMEM((tiles, rows, points), jnp.float32),
        in_specs=[SMEM, VMEM, HBM],
        out_specs=VMEM,
        scratch_shapes=[
            pltpu.VMEM((tiles + 1, rows, points), jnp.float32),
            pltpu.VMEM(blocks.shape, jnp.bfloat16),
            pltpu.SemaphoreType.DMA,
        ],
        compiler_params=KEEP,
        cost_estimate=pl.CostEstimate(
            flops=2 * tiles * blocks.shape[1] * points * points * rows, bytes_accessed=4 << 20, transcendentals=0
        ),
    )(table, placed(state, pltpu.HBM), placed(blocks, pltpu.HBM))


def last_body(before, arrived_ref, local_ref, final_ref, low_ref, high_ref, gathered):
    add_arrived(lambda p: before[LANDED, p], arrived_ref, local_ref, gathered)
    tiles = final_ref.shape[0]
    for t in range(tiles):
        final_ref[t] = gathered[t].astype(jnp.bfloat16)
    low_ref[0] = final_ref[0]
    high_ref[0] = final_ref[tiles - 1]


def last_sum(before, arrived, local):
    tiles, rows, points = local.shape
    return pl.pallas_call(
        last_body,
        out_shape=(
            jax.ShapeDtypeStruct((tiles, rows, points), jnp.bfloat16),
            jax.ShapeDtypeStruct((1, rows, points), jnp.bfloat16),
            jax.ShapeDtypeStruct((1, rows, points), jnp.bfloat16),
        ),
        in_specs=[SMEM, VMEM, VMEM],
        out_specs=(VMEM, VMEM, VMEM),
        scratch_shapes=[
            pltpu.VMEM((tiles + 1, rows, points), jnp.float32),
        ],
        compiler_params=SMALL,
    )(placed(before, pltpu.SMEM), placed(arrived, pltpu.VMEM), placed(local, pltpu.VMEM))


def stretch_tile(ndays, here, dy):
    rows, points = here.shape
    half = rows // 2
    lane = lax.broadcasted_iota(jnp.int32, (rows, points), 1)
    right = pltpu.roll(here, points - 1, 1)
    left = pltpu.roll(here, 1, 1)
    dx = jnp.where(lane == 0, right - here, jnp.where(lane == points - 1, here - left, (right - left) * 0.5))
    a, c = dx[:half], dx[half:]
    b, e = dy[:half], dy[half:]
    c11 = a * a + c * c
    c12 = a * b + c * e
    c22 = b * b + e * e
    gap = c11 - c22
    major = 0.5 * (c11 + c22 + jnp.sqrt(gap * gap + 4.0 * c12 * c12))
    lead = jnp.maximum(major, 1.0)
    det = a * e - b * c
    return jnp.log(lead) / (2.0 * ndays), det * det / lead


def inner_body(ndays, final_ref, ftle_ref, minor_ref):
    tiles, rows, points = final_ref.shape
    for t in range(1, tiles - 1):
        here = final_ref[t].astype(jnp.float32)
        dy = (final_ref[t + 1].astype(jnp.float32) - final_ref[t - 1].astype(jnp.float32)) * 0.5
        at = slice(t * points, (t + 1) * points)
        ftle_ref[:, at], minor_ref[:, at] = stretch_tile(ndays, here, dy)


def edge_body(ndays, final_ref, low_ref, high_ref, ftle_in, minor_in, ftle_ref, minor_ref, ftle_scr, minor_scr, sems):
    tiles, rows, points = final_ref.shape
    copies = []
    for i, t in enumerate((0, tiles - 1)):
        here = final_ref[t].astype(jnp.float32)
        below = (final_ref[t - 1] if t > 0 else low_ref[0]).astype(jnp.float32)
        above = (final_ref[t + 1] if t < tiles - 1 else high_ref[0]).astype(jnp.float32)
        one_sided = above - here if t == 0 else here - below
        at_end = lax.axis_index("tile") == (0 if t == 0 else lax.axis_size("tile") - 1)
        dy = jnp.where(at_end, one_sided, (above - below) * 0.5)
        ftle_scr[i], minor_scr[i] = stretch_tile(ndays, here, dy)
        at = pl.ds(t * points, points)
        for n, (scr, ref) in enumerate(((ftle_scr, ftle_ref), (minor_scr, minor_ref))):
            copy = pltpu.make_async_copy(scr.at[i], ref.at[:, at], sems.at[2 * i + n])
            copy.start()
            copies.append(copy)
    for copy in copies:
        copy.wait()


def stretch_inner(final, ndays):
    tiles, rows, points = final.shape
    shape = jax.ShapeDtypeStruct((rows // 2, tiles * points), jnp.float32)
    return pl.pallas_call(
        functools.partial(inner_body, float(ndays)),
        out_shape=(shape, shape),
        in_specs=[VMEM],
        out_specs=(VMEM, VMEM),
        compiler_params=SMALL,
        cost_estimate=pl.CostEstimate(flops=40 * rows * tiles * points, bytes_accessed=2 << 20, transcendentals=0),
    )(final)


def stretch_edges(final, low, high, inner, ndays):
    tiles, rows, points = final.shape
    shape = jax.ShapeDtypeStruct((rows // 2, tiles * points), jnp.float32)
    scr = pltpu.VMEM((2, rows // 2, points), jnp.float32)
    return pl.pallas_call(
        functools.partial(edge_body, float(ndays)),
        out_shape=(shape, shape),
        in_specs=[VMEM, VMEM, VMEM, HBM, HBM],
        out_specs=(HBM, HBM),
        scratch_shapes=[scr, scr, pltpu.SemaphoreType.DMA((4,))],
        input_output_aliases={3: 0, 4: 1},
        compiler_params=SMALL,
    )(final, low, high, *inner)


def own_rows(dest, me, tiles, peers, nnz):
    off = dest[:, 1:].reshape(tiles * (nnz - 1))
    dev = off // tiles
    stays = dev == me
    home = jnp.where(stays, off % tiles, tiles)
    peer = jnp.arange(peers, dtype=jnp.int32)
    order = jnp.arange(off.shape[0], dtype=jnp.int32)
    free = jnp.logical_not(jnp.any((dev[None, :] == peer[:, None]) & jnp.logical_not(stays)[None, :], axis=1))
    stayed = jnp.sum(jnp.where(order[None, :] < order[:, None], stays[None, :], False).astype(jnp.int32), axis=1)
    frees = jnp.sum(jnp.where(peer[None, :] < peer[:, None], free[None, :], False).astype(jnp.int32), axis=1)
    taken = (stayed[:, None] == frees[None, :]) & free[None, :]
    slot = jnp.where(stays, jnp.sum(jnp.where(taken, peer[None, :], 0), axis=1), dev)
    return slot, home


def body(seeds, blocks, dest_tiles):
    tiles, nnz, points = blocks.shape[1:4]
    width = seeds.shape[2]
    ndays, peers = lax.axis_size("day"), lax.axis_size("tile")
    me = lax.axis_index("tile")
    seeds = seeds.reshape(tiles, points, width)
    wblk = blocks[0]
    onward = functools.partial(lax.ppermute, axis_name="day", perm=shifted(ndays, -1))

    for step in range(ndays):
        if step == 0:
            out, state = send_first(dest_tiles.transpose(2, 0, 1), seeds, wblk, peers)
            dest, state = lax.optimization_barrier((dest_tiles[0], state))
            rows = own_rows(dest, me, tiles, peers, nnz)
            table = jnp.stack([*rows, jnp.zeros_like(rows[0])])
        else:
            out, state = send(quick, arrived, local, off)
        arrived = lax.all_to_all(out, "tile", split_axis=0, concat_axis=0, tiled=True)
        local = keep(table, state, wblk)
        given = table = onward(table)
        if step == 0:
            own = lax.broadcasted_iota(jnp.int32, (peers,), 0) == me
            landed = jnp.where(own, tiles, arrived[:, width, 0].astype(jnp.int32))
            table = jnp.concatenate([table[:2], landed[None]], axis=0)
        if step < ndays - 1:
            wblk = onward(wblk)
            wblk, local = lax.optimization_barrier((wblk, local))
            off, quick = fetch(wblk, table if step else given)
    final, lowest, highest = last_sum(hold(table), arrived, local)
    low = lax.ppermute(highest, "tile", [(i, i + 1) for i in range(peers - 1)])
    high = lax.ppermute(lowest, "tile", [(i + 1, i) for i in range(peers - 1)])
    inner = stretch_inner(final, ndays)
    ftle, minor = stretch_edges(final, low, high, inner, ndays)
    return ftle[None], minor[None]


def solution(mesh):
    in_specs = (P("day", "tile", None), P("day", "tile", None, None, None), P("day", "tile", None))
    out_specs = (P("day", None, "tile"), P("day", None, "tile"))
    return jax.shard_map(body, mesh=mesh, in_specs=in_specs, out_specs=out_specs, check_vma=False)
```
